256 devices in a mesh: section: 2 (over x_hi), patch: 16 (over x_lo, z), head: 8 (over y, core).
Axes of the slice: x: 4 (x_hi: 2, x_lo: 2; x = x_hi * 2 + x_lo), y: 4, z: 8, core: 2. Of those that a mesh axis runs over, the one named last changes fastest.
Arguments:
- latent: float32 [2048, 64], P(('patch', 'head')), may hold values from -6 to 6
- text_states: bfloat16 [2, 512, 3072], P('section', ('patch', 'head')), may hold values from -6 to 6
- img_in: bfloat16 [64, 3072], replicated, may hold values from -0.75 to 0.75
- w_qkv: bfloat16 [2, 3072, 3, 2048], P('section', None, None, 'head'), may hold values from -0.109375 to 0.109375
- w_out: bfloat16 [2, 2048, 3072], P('section', 'head'), may hold values from -4 to 4
- w_final: bfloat16 [3072, 64], replicated, may hold values from -0.109375 to 0.109375
- mod_table: bfloat16 [28, 8, 3072], replicated, may hold values from -3 to 3
- stale_cache: bfloat16 [2, 2048, 2, 2048], P('section', 'patch', None, 'head'), may hold values from -6 to 6
- patch_map: int32 [128], replicated, may hold values from 0 to 127, each once
- timestep: int32 [1], replicated, may hold values from 0 to 26
Outputs:
- velocity: float32 [2, 2048, 64], P('section', ('patch', 'head'))
- next_cache: bfloat16 [2, 2048, 2, 2048], P('section', 'patch', None, 'head')
- text_cache: bfloat16 [2, 512, 2, 2048], P('section', None, None, 'head')
The draws below stay inside these ranges and needn't reach their ends.
Inputs may be any that keep to these rules, and one draw needn't show every extreme that they name: patch_map[g] is the place, counted in blocks of 16 tokens from the start of the image, of the tokens held in block g; each place occurs once.
All inputs are finite; a program needn't handle non-finite values.
Results may differ from the reference program's by a relative error of at most 0.023.
Values may be sent and summed in bfloat16 or wider, within the bound.
No kernel may reach another device: no remote copies, remote signals or barrier semaphores. Data moves between devices by JAX's collectives and lax.ppermute only.
A program may use at most 128 MiB of HBM per device.

```python
import math
import jax
import jax.numpy as jnp
from jax import lax

D = 3072
HEADS = 16
HEAD_DIM = 128
INNER = 2048
CHAN = 64
TEXT = 512
TSTEPS = 28
COLS = 64
STEPS = 2
BLOCKS = 2
MICRO = 2
TOK_DEV = 16
TOK_PATCH = 128
IMAGE = 2048
N_PATCH = 16
N_HEAD = 8


def shard_levels(own_key, shape, pieces, low, top_value):
    gain, own = 1.0, jax.random.fold_in(own_key, 6)
    for axis_at, parts in pieces:
        draws = jnp.exp(jax.random.uniform(jax.random.fold_in(own, axis_at), (parts,), jnp.float32, low / len(pieces), top_value / len(pieces)))
        gain = gain * jnp.repeat(draws, shape[axis_at] // parts).reshape([-1 if axis == axis_at else 1 for axis in range(len(shape))])
    return gain


def bell_draw(key, dims, scale, reach, pieces=(), held_as=jnp.bfloat16):
    drawn = jax.random.normal(key, dims, jnp.float32) * scale
    if len(pieces) > 0:
        drawn = shard_levels(key, dims, pieces, -0.22, 0.18) * drawn
    return jnp.clip(drawn, min=-reach, max=reach).astype(held_as)


def setup_inputs(seed: int = 0) -> dict:
    key_list = jax.random.split(jax.random.key(seed), 11)
    return {
        "latent": bell_draw(key_list[0], (IMAGE, CHAN), 1.0, 6.0, ((0, 128),), jnp.float32),
        "text_states": bell_draw(key_list[1], (BLOCKS, TEXT, D), 1.0, 6.0, ((0, 2), (1, 128))),
        "img_in": bell_draw(key_list[2], (CHAN, D), CHAN ** -0.5, 0.75),
        "w_qkv": bell_draw(key_list[3], (BLOCKS, D, 3, INNER), D ** -0.5, 0.109375, ((0, 2), (3, 8))),
        "w_out": bell_draw(key_list[4], (BLOCKS, INNER, D), 2 ** -0.5, 4.0, ((0, 2), (1, 8))),
        "w_final": bell_draw(key_list[5], (D, CHAN), D ** -0.5, 0.109375),
        "mod_table": bell_draw(key_list[6], (TSTEPS, 3 * BLOCKS + 2, D), 0.5, 3.0),
        "stale_cache": bell_draw(key_list[7], (BLOCKS, IMAGE, 2, INNER), 1.0, 6.0, ((0, 2), (1, 16), (3, 8))),
        "patch_map": jax.random.permutation(key_list[8], N_PATCH * N_HEAD).astype(jnp.int32),
        "timestep": jax.random.randint(key_list[9], (1,), 0, TSTEPS - 1).astype(jnp.int32),
    }


EPSILON = 1e-06

def layer_norm(values):
    mean_value = lax.optimization_barrier(jnp.mean(values, -1, keepdims=True))
    centred = values - mean_value
    variance = lax.optimization_barrier(jnp.mean(centred * centred, -1, keepdims=True))
    return centred / jnp.sqrt(variance + EPSILON)

def modulate(hidden, shift_row, scale_row):
    return (layer_norm(hidden.astype(jnp.float32)) * (1.0 + scale_row) + shift_row).astype(jnp.bfloat16)

def grid_angles(grid_rows, columns, head_width):
    pairs_all = head_width // 2
    fixed_pairs = pairs_all // 8
    row_pairs = (pairs_all - fixed_pairs) // 2
    col_pairs = pairs_all - fixed_pairs - row_pairs
    pair_index = jnp.arange(pairs_all).astype(jnp.float32)
    row_freq = jnp.where((pair_index >= fixed_pairs) & (pair_index < fixed_pairs + row_pairs), 10000.0 ** (-(pair_index - fixed_pairs) / row_pairs), 0.0)
    col_freq = jnp.where(pair_index >= fixed_pairs + row_pairs, 10000.0 ** (-(pair_index - fixed_pairs - row_pairs) / col_pairs), 0.0)
    return grid_rows[:, None] * row_freq[None, :] + columns[:, None] * col_freq[None, :]

def qk_norm(values, angles):
    values = values.astype(jnp.float32)
    values = values / jnp.sqrt(lax.optimization_barrier(jnp.mean(values * values, -1, keepdims=True)) + EPSILON)
    half_dim = values.shape[-1] // 2
    cosine = jnp.cos(angles)[:, None, :]
    sine_part = jnp.sin(angles)[:, None, :]
    leading = values[..., :half_dim]
    trailing = values[..., half_dim:]
    return jnp.concatenate([leading * cosine - trailing * sine_part, trailing * cosine + leading * sine_part], -1).astype(jnp.bfloat16)

def sigma_of(roster):
    fraction = 1.0 - roster.astype(jnp.float32) / TSTEPS
    return 3.0 * fraction / (1.0 + 2.0 * fraction)

def attend(queries, all_keys, all_values):
    scores = jnp.einsum('qhd,khd->qhk', queries.astype(jnp.float32), all_keys.astype(jnp.float32)) * (1.0 / math.sqrt(HEAD_DIM))
    weights = jnp.exp(scores)
    totals = lax.optimization_barrier(jnp.sum(weights, -1))
    weights_b = weights.astype(jnp.bfloat16)
    summed = jnp.einsum('qhk,khd->qhd', weights_b.astype(jnp.float32), all_values.astype(jnp.float32))
    return summed / totals[..., None]

def reference(latent, text_states, img_in, w_qkv, w_out, w_final, mod_table, stale_cache, patch_map, timestep):
    micro_rows = TOK_DEV // MICRO
    tokens = jnp.arange(IMAGE, dtype=jnp.int32)
    patch_of = tokens // TOK_PATCH
    block_of = tokens // TOK_DEV
    places = patch_map[block_of] * TOK_DEV + tokens % TOK_DEV
    grid_rows = (places // COLS).astype(jnp.float32)
    columns = (places % COLS).astype(jnp.float32)
    angles = grid_angles(grid_rows, columns, HEAD_DIM)
    text_angles = jnp.zeros((TEXT, HEAD_DIM // 2), jnp.float32)
    micro_of = tokens % TOK_DEV // micro_rows
    first_step = timestep[0]
    step_size = sigma_of(first_step + 1) - sigma_of(first_step)
    latent_now = latent
    stale = stale_cache
    velocities = []
    text_blocks = []
    for denoise in range(STEPS):
        mod_rows = lax.dynamic_index_in_dim(mod_table, first_step + denoise, 0, keepdims=False).astype(jnp.float32)
        hidden = jnp.dot(latent_now.astype(jnp.bfloat16), img_in, preferred_element_type=jnp.float32).astype(jnp.bfloat16)
        fresh_blocks = []
        text_blocks = []
        for block_index in range(BLOCKS):
            shift_row = mod_rows[3 * block_index]
            scale_row = mod_rows[3 * block_index + 1]
            gate_row = mod_rows[3 * block_index + 2]
            weight = w_qkv[block_index].reshape(D, 3 * INNER)
            projected = jnp.dot(modulate(hidden, shift_row, scale_row), weight, preferred_element_type=jnp.float32).reshape(IMAGE, 3, HEADS, HEAD_DIM)
            queries = qk_norm(projected[:, 0], angles)
            fresh_key = projected[:, 1].astype(jnp.bfloat16)
            fresh_value = projected[:, 2].astype(jnp.bfloat16)
            fresh_keys = qk_norm(fresh_key, angles)
            old_pairs = stale[block_index].reshape(IMAGE, 2, HEADS, HEAD_DIM)
            stale_keys = qk_norm(old_pairs[:, 0], angles)
            stale_values = old_pairs[:, 1]
            text_proj = jnp.dot(modulate(text_states[block_index], shift_row, scale_row), weight[:, INNER:], preferred_element_type=jnp.float32).reshape(TEXT, 2, HEADS, HEAD_DIM)
            text_keys = qk_norm(text_proj[:, 0], text_angles)
            text_values = text_proj[:, 1].astype(jnp.bfloat16)
            text_blocks.append(jnp.stack([text_keys.reshape(TEXT, INNER), text_values.reshape(TEXT, INNER)], 1))
            grouped = queries.reshape(N_PATCH, N_HEAD, MICRO, micro_rows, HEADS, HEAD_DIM)

            def per_patch(patch_idx):
                owned = patch_of == patch_idx
                patch_queries = lax.dynamic_index_in_dim(grouped, patch_idx, 0, keepdims=False)
                results = []
                for micro_idx in range(MICRO):
                    use_fresh = (owned & (micro_of <= micro_idx))[:, None, None]
                    all_keys = jnp.concatenate([text_keys, jnp.where(use_fresh, fresh_keys, stale_keys)], 0)
                    all_values = jnp.concatenate([text_values, jnp.where(use_fresh, fresh_value, stale_values)], 0)
                    rows_now = patch_queries[:, micro_idx].reshape(N_HEAD * micro_rows, HEADS, HEAD_DIM)
                    results.append(attend(rows_now, all_keys, all_values).reshape(N_HEAD, micro_rows, INNER))
                return jnp.stack(results, 1).reshape(TOK_PATCH, INNER).astype(jnp.bfloat16)
            attended = lax.map(per_patch, jnp.arange(N_PATCH, dtype=jnp.int32)).reshape(IMAGE, INNER)
            mixed = jnp.dot(attended, w_out[block_index], preferred_element_type=jnp.float32)
            hidden = (hidden.astype(jnp.float32) + gate_row * mixed).astype(jnp.bfloat16)
            fresh_blocks.append(jnp.stack([fresh_key.reshape(IMAGE, INNER), fresh_value.reshape(IMAGE, INNER)], 1))
        velocity = jnp.dot(modulate(hidden, mod_rows[3 * BLOCKS], mod_rows[3 * BLOCKS + 1]), w_final, preferred_element_type=jnp.float32)
        velocities.append(velocity)
        latent_now = latent_now + step_size * velocity
        stale = jnp.stack(fresh_blocks, 0)
    return (jnp.stack(velocities, 0), stale, jnp.stack(text_blocks, 0))
```

```python
import math

import jax
import jax.numpy as jnp
import numpy as np
from jax import lax
from jax.experimental import pallas as pl
from jax.experimental.pallas import tpu as pltpu
from jax.sharding import PartitionSpec as P

HEAD_DIM = 128
TSTEPS = 28
COLS = 64
STEPS = 2
BLOCKS = 2
MICRO = 2
EPSILON = 1e-06
F32 = jnp.float32
BF16 = jnp.bfloat16
N_Y = 4
N_Z = 8


def call(body, outs, *args):
    single = not isinstance(outs, list)
    shapes = [outs] if single else outs
    result = pl.pallas_call(
        body,
        out_shape=[jax.ShapeDtypeStruct(shape, dtype) for shape, dtype in shapes],
        in_specs=[pl.BlockSpec(memory_space=pltpu.VMEM)] * len(args),
        out_specs=[pl.BlockSpec(memory_space=pltpu.VMEM)] * len(shapes),
        compiler_params=pltpu.CompilerParams(vmem_limit_bytes=28 * 1024 * 1024),
    )(*args)
    return result[0] if single else result


def permuted(shard, axis, target):
    length = lax.axis_size(axis)
    return lax.ppermute(shard, axis, [(i, target(i)) for i in range(length)])


def along_y(shard, by):
    return permuted(shard, "head", lambda i: (((i >> 1) + by) % N_Y) * 2 + (i & 1))


def other_core(shard):
    return permuted(shard, "head", lambda i: i ^ 1)


def along_z(shard, by):
    return permuted(shard, "patch", lambda i: (i & N_Z) | ((i + by) % N_Z))


def other_row(shard):
    return permuted(shard, "patch", lambda i: i ^ N_Z)


def gathered_heads(rows):
    half = jnp.concatenate([rows] + [along_y(rows, by) for by in (1, 2, 3)], 0)
    return half, other_core(half)


def layer_norm(values):
    centred = values - jnp.mean(values, -1, keepdims=True)
    variance = jnp.mean(centred * centred, -1, keepdims=True)
    return centred / jnp.sqrt(variance + EPSILON)


def modulated(values, shift_row, scale_row):
    return layer_norm(values.astype(F32)) * (1.0 + scale_row) + shift_row


def rotated(values, cosine, sine):
    values = values / jnp.sqrt(jnp.mean(values * values, -1, keepdims=True) + EPSILON)
    half = HEAD_DIM // 2
    swapped = jnp.concatenate([values[:, half:], values[:, :half]], -1)
    return values * cosine + swapped * sine


def each_head(values, change):
    heads = values.shape[-1] // HEAD_DIM
    return jnp.concatenate(
        [change(values[:, h * HEAD_DIM : (h + 1) * HEAD_DIM]) for h in range(heads)], -1
    )


def stale_body(stale_ref, cos_ref, sin_ref, out_ref):
    inner = stale_ref.shape[1] // 2
    cosine, sine = cos_ref[...], sin_ref[...]
    keys = each_head(stale_ref[:, :inner].astype(F32), lambda v: rotated(v, cosine, sine))
    out_ref[:, :inner] = keys.astype(BF16)
    out_ref[:, inner:] = stale_ref[:, inner:]


def first_rows_body(latent_ref, text_ref, img_ref, mods_ref, rows_ref, hidden_ref):
    hidden = jnp.dot(latent_ref[...].astype(BF16), img_ref[...], preferred_element_type=F32)
    hidden = hidden.astype(BF16)
    hidden_ref[...] = hidden
    normed = modulated(hidden, mods_ref[0, 0:1], mods_ref[0, 1:2])
    still = layer_norm(text_ref[...].astype(F32))
    texts = [still * (1.0 + mods_ref[k, 1:2]) + mods_ref[k, 0:1] for k in range(STEPS)]
    rows_ref[...] = jnp.concatenate([normed] + texts, 0).astype(BF16)


def entry_body(latent_ref, velocity_ref, step_ref, img_ref, mods_ref, rows_ref, hidden_ref):
    latent_now = latent_ref[...] + step_ref[0:1, 0:1] * velocity_ref[...]
    hidden = jnp.dot(latent_now.astype(BF16), img_ref[...], preferred_element_type=F32)
    hidden = hidden.astype(BF16)
    hidden_ref[...] = hidden
    rows_ref[...] = modulated(hidden, mods_ref[0:1], mods_ref[1:2]).astype(BF16)


def normed_body(hidden_ref, mods_ref, rows_ref):
    rows_ref[...] = modulated(hidden_ref[...], mods_ref[0:1], mods_ref[1:2]).astype(BF16)


def image_parts(projected, cosine, sine, q_ref, pairs_ref, raw_ref):
    inner = projected.shape[1] // 3
    q_ref[...] = each_head(
        projected[:, :inner], lambda v: rotated(v, cosine, sine)
    ).astype(BF16)
    raw = projected[:, inner:].astype(BF16)
    raw_ref[...] = raw
    keys = each_head(raw[:, :inner].astype(F32), lambda v: rotated(v, cosine, sine))
    pairs_ref[:, :inner] = keys.astype(BF16)
    pairs_ref[:, inner:] = raw[:, inner:]


def first_project_body(
    half_ref, other_ref, w_ref, cos_ref, sin_ref, order_ref, q_ref, pairs_ref, raw_ref, t0_ref, t1_ref
):
    rows = jnp.concatenate([half_ref[...], other_ref[...]], 0)
    projected = jnp.dot(rows, w_ref[...], preferred_element_type=F32)
    inner = projected.shape[1] // 3
    own = q_ref.shape[0] // 8
    texts = rows.shape[0] // 8 - own
    image = jnp.concatenate(
        [projected[i * (own + texts) : i * (own + texts) + own] for i in range(8)], 0
    )
    image_parts(image, cos_ref[...], sin_ref[...], q_ref, pairs_ref, raw_ref)
    text = jnp.concatenate(
        [projected[i * (own + texts) + own : (i + 1) * (own + texts), inner:] for i in range(8)], 0
    )
    keys = each_head(
        text[:, :inner],
        lambda v: v / jnp.sqrt(jnp.mean(v * v, -1, keepdims=True) + EPSILON),
    )
    pairs = jnp.concatenate([keys, text[:, inner:]], -1).astype(BF16)
    pairs = jnp.dot(order_ref[...], pairs, preferred_element_type=F32).astype(BF16)
    count = pairs.shape[0] // 2
    t0_ref[...] = pairs[:count]
    t1_ref[...] = pairs[count:]


def project_body(half_ref, other_ref, w_ref, cos_ref, sin_ref, q_ref, pairs_ref, raw_ref):
    rows = jnp.concatenate([half_ref[...], other_ref[...]], 0)
    projected = jnp.dot(rows, w_ref[...], preferred_element_type=F32)
    image_parts(projected, cos_ref[...], sin_ref[...], q_ref, pairs_ref, raw_ref)


def attend_body(q_ref, pairs_ref, stale_ref, wo_ref, *refs):
    far_refs, (keep_ref, send_ref) = refs[:-2], refs[-2:]
    count, inner = q_ref.shape
    scale = 1.0 / math.sqrt(HEAD_DIM)
    half_rows = 2 * 8
    row_micro = lax.broadcasted_iota(jnp.int32, (count, count), 0) % half_rows // 8
    key_micro = lax.broadcasted_iota(jnp.int32, (count, count), 1) % half_rows // 8
    blocks = [(ref, None) for ref in far_refs]
    blocks += [(pairs_ref, key_micro <= row_micro), (stale_ref, key_micro > row_micro)]
    done = []
    for h in range(inner // HEAD_DIM):
        lo, hi = h * HEAD_DIM, (h + 1) * HEAD_DIM
        queries = q_ref[:, lo:hi]
        total = jnp.zeros((count, 1), F32)
        summed = jnp.zeros((count, HEAD_DIM), F32)
        for ref, mask in blocks:
            scores = lax.dot_general(
                queries, ref[:, lo:hi], (((1,), (1,)), ((), ())), preferred_element_type=F32
            )
            weights = jnp.exp(scores * scale)
            if mask is not None:
                weights = jnp.where(mask, weights, 0.0)
            total = total + jnp.sum(weights, -1, keepdims=True)
            summed = summed + jnp.dot(
                weights.astype(BF16), ref[:, inner + lo : inner + hi], preferred_element_type=F32
            )
        done.append((summed / total).astype(BF16))
    attended = jnp.concatenate(done, -1)
    mixed = jnp.dot(attended, wo_ref[...], preferred_element_type=F32).astype(BF16)
    keep_ref[...] = mixed[: count // 2]
    send_ref[...] = mixed[count // 2 :]


def cores_body(keep_ref, came_ref, *out_refs):
    own = out_refs[0].shape[0]
    for s, ref in enumerate(out_refs):
        at = pl.ds(s * own, own)
        ref[...] = (keep_ref[at].astype(F32) + came_ref[at].astype(F32)).astype(BF16)


def mixed_hidden(part_refs, hidden_ref, gate_row):
    mixed = part_refs[0][...].astype(F32)
    for ref in part_refs[1:]:
        mixed = mixed + ref[...].astype(F32)
    return (hidden_ref[...].astype(F32) + gate_row * mixed).astype(BF16)


def hidden_body(a_ref, b_ref, c_ref, d_ref, hidden_ref, mods_ref, out_ref):
    out_ref[...] = mixed_hidden([a_ref, b_ref, c_ref, d_ref], hidden_ref, mods_ref[2:3])


def velocity_body(hidden_ref, finals_ref, w_ref, out_ref):
    rows = modulated(hidden_ref[...], finals_ref[0:1], finals_ref[1:2]).astype(BF16)
    out_ref[...] = jnp.dot(rows, w_ref[...], preferred_element_type=F32)


def sigma_of(roster):
    fraction = 1.0 - roster.astype(F32) / TSTEPS
    return 3.0 * fraction / (1.0 + 2.0 * fraction)


def angle_parts(places):
    pairs_all = HEAD_DIM // 2
    fixed = pairs_all // 8
    row_pairs = (pairs_all - fixed) // 2
    col_pairs = pairs_all - fixed - row_pairs
    index = np.arange(pairs_all, dtype=np.float64)
    row_freq = np.zeros(pairs_all)
    col_freq = np.zeros(pairs_all)
    row_freq[fixed : fixed + row_pairs] = 10000.0 ** (-np.arange(row_pairs) / row_pairs)
    col_freq[fixed + row_pairs :] = 10000.0 ** (-np.arange(col_pairs) / col_pairs)
    two = lambda freq: np.concatenate([freq, freq]).astype(np.float32)[None, :]
    angles = (places // COLS).astype(F32)[:, None] * two(row_freq) + (places % COLS).astype(F32)[
        :, None
    ] * two(col_freq)
    sign = np.where(np.arange(HEAD_DIM) < pairs_all, -1.0, 1.0).astype(np.float32)[None, :]
    return jnp.cos(angles), jnp.sin(angles) * sign


def ring_parts(pairs, own_text):
    rows = jnp.concatenate([pairs, own_text], 0)
    count = rows.shape[0]
    there = other_row(rows)
    both = jnp.concatenate([rows, there], 0)
    up = down = both
    parts = [there]
    for _ in range(N_Z // 2 - 1):
        up, down = along_z(up, 1), along_z(down, -1)
        parts += [up, down]
    parts += [along_z(up[:count], 1), along_z(down[count:], -1)]
    return tuple(parts)


def first_ring(pairs, own_text):
    count = pairs.shape[0]
    there = other_row(pairs)
    both = jnp.concatenate([pairs, there], 0)
    up1, down1 = along_z(both, 1), along_z(both, -1)
    up2, down2 = along_z(up1, 1), along_z(down1, -1)
    text_there = other_row(own_text)
    texts = jnp.concatenate([own_text, text_there], 0)
    t_count = texts.shape[0]
    up3 = along_z(jnp.concatenate([up2, texts], 0), 1)
    down3 = along_z(jnp.concatenate([texts, down2], 0), -1)
    up4, down4 = along_z(up3[count:], 1), along_z(down3[: t_count + count], -1)
    up5, down5 = along_z(up4[count:], 1), along_z(down4[:t_count], -1)
    up6 = along_z(up5[: t_count // 2], 1)
    down6 = along_z(down5[t_count // 2 :], -1)
    return [there, up1, down1, up2, down2, up3, down3, up4, down4]+[text_there, up5, down5, up6, down6]


def per_device(
    latent, text_states, img_in, w_qkv, w_out, w_final, mod_table, stale_cache, patch_map, timestep
):
    section = lax.axis_index("section")
    patch = lax.axis_index("patch")
    head = lax.axis_index("head")
    tok_dev, chan = latent.shape
    n_head = lax.axis_size("head")
    n_patch = lax.axis_size("patch")
    tok_patch = tok_dev * n_head
    width = img_in.shape[1]
    inner = w_out.shape[1]
    text_dev = text_states.shape[1]
    text_patch = text_dev * n_head
    first_step = timestep[0]
    step_size = (sigma_of(first_step + 1) - sigma_of(first_step)).reshape(1, 1)
    mod_rows = lax.dynamic_slice_in_dim(mod_table, first_step, STEPS, 0).astype(F32)
    mods = lax.dynamic_slice_in_dim(mod_rows, 3 * section, 3, 1)
    finals = mod_rows[:, 3 * BLOCKS : 3 * BLOCKS + 2]
    weight = w_qkv[0].reshape(width, 3 * inner)
    wo_local = w_out[0]

    y_at, core = head // 2, head % 2
    own_map = lax.dynamic_slice_in_dim(patch_map, patch * n_head, n_head, 0)

    def head_of(block):
        return (y_at - block % N_Y) % N_Y * 2 + (core + block // N_Y) % 2

    in_patch = jnp.arange(tok_patch, dtype=jnp.int32)
    heads_rel = head_of(in_patch // tok_dev)
    heads_both = jnp.concatenate([in_patch // tok_dev, heads_rel])
    places = jnp.sum(
        jnp.where(heads_both[:, None] == jnp.arange(n_head)[None, :], own_map[None, :], 0), -1
    ) * tok_dev + jnp.concatenate([in_patch, in_patch]) % tok_dev
    cos_both, sin_both = angle_parts(places)
    cos_abs, sin_abs = cos_both[:tok_patch], sin_both[:tok_patch]
    cos_rel, sin_rel = cos_both[tok_patch:], sin_both[tok_patch:]
    image_order = (
        (heads_rel * tok_dev + in_patch % tok_dev)[None, :] == in_patch[:, None]
    ).astype(BF16)
    text_at = jnp.arange(STEPS * text_patch, dtype=jnp.int32)
    in_text = text_at % (STEPS * text_dev)
    text_to = (
        in_text // text_dev * text_patch
        + head_of(text_at // (STEPS * text_dev)) * text_dev
        + in_text % text_dev
    )
    text_order = (text_to[None, :] == text_at[:, None]).astype(BF16)

    stale_own = call(
        stale_body,
        ((tok_patch, 2 * inner), BF16),
        stale_cache[0].reshape(tok_patch, 2 * inner),
        cos_abs,
        sin_abs,
    )
    first_rows, hidden = call(
        first_rows_body,
        [((tok_dev + STEPS * text_dev, width), BF16), ((tok_dev, width), BF16)],
        latent,
        text_states[0],
        img_in,
        mods,
    )
    half, other = gathered_heads(first_rows)
    pair_shape = ((tok_patch, 2 * inner), BF16)
    text_shape = ((text_patch, 2 * inner), BF16)
    queries, pairs, raw, text0, text1 = call(
        first_project_body,
        [((tok_patch, inner), BF16), pair_shape, pair_shape, text_shape, text_shape],
        half,
        other,
        weight,
        cos_rel,
        sin_rel,
        text_order,
    )
    far = first_ring(stale_own, text0) + [text0]

    def attend(queries, pairs, stale_pairs, far, hidden, gate_mods):
        keep, send = call(
            attend_body,
            [((tok_patch // 2, width), BF16)] * 2,
            queries,
            pairs,
            stale_pairs,
            wo_local,
            *far,
        )
        parts = call(cores_body, [((tok_dev, width), BF16)] * N_Y, keep, other_core(send))
        parts = [parts[0]] + [along_y(parts[by], -by) for by in (1, 2, 3)]
        return call(hidden_body, ((tok_dev, width), BF16), *parts, hidden, gate_mods)

    def stage(rows, hidden, stale_pairs, far, gate_mods):
        half, other = gathered_heads(rows)
        queries, pairs, raw = call(
            project_body,
            [((tok_patch, inner), BF16), pair_shape, pair_shape],
            half,
            other,
            weight,
            cos_rel,
            sin_rel,
        )
        return attend(queries, pairs, stale_pairs, far, hidden, gate_mods), pairs, raw

    def to_next(hidden):
        return lax.ppermute(hidden, "section", [(0, 1)])

    def normed_rows(hidden, mods_now):
        return call(normed_body, ((tok_dev, width), BF16), hidden, mods_now)

    def empty_parts():
        count = tok_patch + text_patch
        one = jnp.zeros((count, 2 * inner), BF16)
        two = jnp.zeros((2 * count, 2 * inner), BF16)
        return (one,) + (two,) * (2 * (N_Z // 2 - 1)) + (one, one)

    at_first = section == 0
    hidden0 = lax.cond(
        at_first,
        lambda: attend(queries, pairs, stale_own, far, hidden, mods[0]),
        lambda: hidden,
    )
    hidden_in = to_next(hidden0)
    rows = normed_rows(hidden_in, mods[0])
    hidden1, pairs = lax.cond(
        at_first,
        lambda: (hidden_in, pairs),
        lambda: stage(rows, hidden_in, stale_own, far, mods[0])[:2],
    )
    far = lax.cond(at_first, lambda: ring_parts(pairs, text1), empty_parts)
    velocity0 = call(velocity_body, ((tok_dev, chan), F32), hidden1, finals[0], w_final)
    velocity_back = lax.ppermute(velocity0, "section", [(1, 0)])
    rows, hidden = call(
        entry_body,
        [((tok_dev, width), BF16)] * 2,
        latent,
        velocity_back,
        step_size,
        img_in,
        mods[1],
    )
    far_second = lax.cond(at_first, empty_parts, lambda: ring_parts(pairs, text1))
    hidden2, raw = lax.cond(
        at_first,
        lambda: stage(rows, hidden, pairs, far + (text1,), mods[1])[::2],
        lambda: (hidden, pairs),
    )
    hidden_in = to_next(hidden2)
    rows = normed_rows(hidden_in, mods[1])
    hidden3, raw = lax.cond(
        at_first,
        lambda: (hidden_in, raw),
        lambda: stage(rows, hidden_in, pairs, far_second + (text1,), mods[1])[::2],
    )
    velocity1 = call(velocity_body, ((tok_dev, chan), F32), hidden3, finals[1], w_final)

    velocity_out = jnp.where(at_first, velocity_back, velocity1)[None]
    cache_out = jnp.dot(image_order, raw, preferred_element_type=F32).astype(BF16)
    far_last = [jnp.where(at_first, a, b) for a, b in zip(far, far_second)]
    text_parts = [text1]
    for part in far_last:
        for at in range(0, part.shape[0], tok_patch + text_patch):
            text_parts.append(part[at + tok_patch : at + tok_patch + text_patch])
    z_at, row_at = patch % N_Z, patch // N_Z
    sources = [(0, 0), (0, 1)]
    for by in range(1, N_Z // 2):
        sources += [(-by, 0), (-by, 1), (by, 0), (by, 1)]
    sources += [(N_Z // 2, 0), (N_Z // 2, 1)]
    text_out = jnp.zeros((n_patch * text_patch, 2 * inner), BF16)
    for part, (by, row) in zip(text_parts, sources):
        source = (row_at + row) % 2 * N_Z + (z_at + by) % N_Z
        text_out = lax.dynamic_update_slice_in_dim(text_out, part, source * text_patch, 0)
    return (
        velocity_out,
        cache_out.reshape(1, tok_patch, 2, inner),
        text_out.reshape(1, n_patch * text_patch, 2, inner),
    )


def solution(mesh):
    return jax.shard_map(
        per_device,
        mesh=mesh,
        in_specs=(
            P(("patch", "head"), None),
            P("section", ("patch", "head"), None),
            P(),
            P("section", None, None, "head"),
            P("section", "head", None),
            P(),
            P(),
            P("section", "patch", None, "head"),
            P(),
            P(),
        ),
        out_specs=(
            P("section", ("patch", "head"), None),
            P("section", "patch", None, "head"),
            P("section", None, None, "head"),
        ),
        check_vma=False,
    )
```

```python
import functools
import math

import jax
import jax.numpy as jnp
import numpy as np
from jax import lax
from jax.experimental import pallas as pl
from jax.experimental.pallas import tpu as pltpu
from jax.sharding import PartitionSpec as P

HEAD_DIM = 128
TSTEPS = 28
COLS = 64
STEPS = 2
BLOCKS = 2
MICRO = 2
EPSILON = 1e-06
F32 = jnp.float32
BF16 = jnp.bfloat16
N_Y = 4
N_Z = 8


VMEM = pl.BlockSpec(memory_space=pltpu.VMEM)
SMEM = pl.BlockSpec(memory_space=pltpu.SMEM)
HBM = pl.BlockSpec(memory_space=pltpu.HBM)


def call(body, outs, *args, specs=None, scratch=(), vmem=16):
    single = not isinstance(outs, list)
    shapes = [outs] if single else outs
    result = pl.pallas_call(
        body,
        out_shape=[jax.ShapeDtypeStruct(shape, dtype) for shape, dtype in shapes],
        in_specs=[VMEM] * len(args) if specs is None else specs,
        out_specs=[VMEM] * len(shapes),
        scratch_shapes=list(scratch),
        compiler_params=pltpu.CompilerParams(vmem_limit_bytes=vmem * 1024 * 1024),
    )(*args)
    return result[0] if single else result


def unset(shapes):
    return list(pl.pallas_call(
        lambda *refs: None,
        out_shape=[jax.ShapeDtypeStruct(shape, BF16) for shape in shapes],
        out_specs=[pl.BlockSpec(memory_space=pl.ANY)] * len(shapes),
    )())


def permuted(shard, axis, target):
    length = lax.axis_size(axis)
    return lax.ppermute(shard, axis, [(i, target(i)) for i in range(length)])


def along_y(shard, by):
    return permuted(shard, "head", lambda i: (((i >> 1) + by) % N_Y) * 2 + (i & 1))


def other_core(shard):
    return permuted(shard, "head", lambda i: i ^ 1)


def along_z(shard, by):
    return permuted(shard, "patch", lambda i: (i & N_Z) | ((i + by) % N_Z))


def other_row(shard):
    return permuted(shard, "patch", lambda i: i ^ N_Z)


def gathered_heads(rows):
    half = jnp.concatenate([rows] + [along_y(rows, by) for by in (1, 2, 3)], 0)
    return half, other_core(half)


def layer_norm(values):
    centred = values - jnp.mean(values, -1, keepdims=True)
    variance = jnp.mean(centred * centred, -1, keepdims=True)
    return centred / jnp.sqrt(variance + EPSILON)


def modulated(values, shift_row, scale_row):
    return layer_norm(values.astype(F32)) * (1.0 + scale_row) + shift_row


def rotated(values, cosine, sine):
    values = values / jnp.sqrt(jnp.mean(values * values, -1, keepdims=True) + EPSILON)
    half = HEAD_DIM // 2
    swapped = jnp.concatenate([values[:, half:], values[:, :half]], -1)
    return values * cosine + swapped * sine


def each_head(values, change):
    heads = values.shape[-1] // HEAD_DIM
    return jnp.concatenate(
        [change(values[:, h * HEAD_DIM : (h + 1) * HEAD_DIM]) for h in range(heads)], -1
    )


def head_at(block, y_at, core):
    return lax.rem(y_at - block % N_Y + N_Y, N_Y) * 2 + lax.rem(core + block // N_Y, 2)


def frequencies():
    pairs_all = HEAD_DIM // 2
    fixed = pairs_all // 8
    row_pairs = (pairs_all - fixed) // 2
    col_pairs = pairs_all - fixed - row_pairs
    lane = lax.broadcasted_iota(jnp.int32, (1, HEAD_DIM), 1)
    pair = lane % pairs_all
    base = -math.log2(10000.0)
    row_freq = jnp.exp2((pair - fixed).astype(F32) * (base / row_pairs))
    col_freq = jnp.exp2((pair - fixed - row_pairs).astype(F32) * (base / col_pairs))
    in_rows = (pair >= fixed) & (pair < fixed + row_pairs)
    return (
        jnp.where(in_rows, row_freq, 0.0),
        jnp.where(pair >= fixed + row_pairs, col_freq, 0.0),
        jnp.where(lane < pairs_all, -1.0, 1.0),
    )


def prelude_body(
    step_ref,
    map_ref,
    stale_ref,
    latent_hbm,
    text_hbm,
    img_hbm,
    table_hbm,
    pairs_ref,
    rows_ref,
    hidden_ref,
    mods_ref,
    cos_ref,
    sin_ref,
    latent_ref,
    text_ref,
    img_ref,
    table_ref,
    sems,
):
    copies = [
        pltpu.make_async_copy(src, dst, sems.at[i])
        for i, (src, dst) in enumerate(
            [
                (table_hbm.at[pl.ds(step_ref[0], STEPS)], table_ref),
                (latent_hbm, latent_ref),
                (img_hbm, img_ref),
                (text_hbm, text_ref),
            ]
        )
    ]
    for copy in copies:
        copy.start()
    section, patch, head = (lax.axis_index(a) for a in ("section", "patch", "head"))
    y_at, core = lax.div(head, 2), lax.rem(head, 2)
    tok_dev = latent_ref.shape[0]
    row_freq, col_freq, sign = frequencies()
    in_block = lax.broadcasted_iota(jnp.int32, (tok_dev, HEAD_DIM), 0).astype(F32)

    def tables(head_now):
        place = map_ref[patch * 8 + head_now] * tok_dev
        grid_row = lax.div(place, COLS).astype(F32)
        column = lax.rem(place, COLS).astype(F32) + in_block
        angles = grid_row * row_freq + column * col_freq
        return jnp.cos(angles), jnp.sin(angles) * sign

    inner = stale_ref.shape[1] // 2
    for block in range(8):
        head_now = head_at(block, y_at, core)
        cosine, sine = tables(head_now)
        at = pl.ds(block * tok_dev, tok_dev)
        cos_ref[at] = cosine
        sin_ref[at] = sine
        there = pl.ds(pl.multiple_of(head_now * tok_dev, tok_dev), tok_dev)
        keys = each_head(stale_ref[there, :inner].astype(F32), lambda v: rotated(v, cosine, sine))
        pairs_ref[at, :inner] = keys.astype(BF16)
        pairs_ref[at, inner:] = stale_ref[there, inner:]
    for copy in copies:
        copy.wait()
    for k in range(STEPS):
        table = table_ref[k].astype(F32)
        mods_ref[k, 0:3] = jnp.where(section == 0, table[0:3], table[3:6])
        mods_ref[k, 3:5] = table[6:8]
    hidden = jnp.dot(latent_ref[...].astype(BF16), img_ref[...], preferred_element_type=F32)
    hidden = hidden.astype(BF16)
    hidden_ref[...] = hidden
    normed = modulated(hidden, mods_ref[0, 0:1], mods_ref[0, 1:2])
    still = layer_norm(text_ref[...].astype(F32))
    texts = [still * (1.0 + mods_ref[k, 1:2]) + mods_ref[k, 0:1] for k in range(STEPS)]
    rows_ref[...] = jnp.concatenate([normed] + texts, 0).astype(BF16)


def entry_body(latent_ref, velocity_ref, step_ref, img_ref, mods_ref, rows_ref, hidden_ref):
    first = step_ref[0].astype(F32)
    sigmas = []
    for roster in (first, first + 1.0):
        fraction = 1.0 - jnp.full(latent_ref.shape, roster) / TSTEPS
        sigmas.append(3.0 * fraction / (1.0 + 2.0 * fraction))
    latent_now = latent_ref[...] + (sigmas[1] - sigmas[0]) * velocity_ref[...]
    hidden = jnp.dot(latent_now.astype(BF16), img_ref[...], preferred_element_type=F32)
    hidden = hidden.astype(BF16)
    hidden_ref[...] = hidden
    rows_ref[...] = modulated(hidden, mods_ref[1, 0:1], mods_ref[1, 1:2]).astype(BF16)


def normed_body(k, hidden_ref, mods_ref, rows_ref):
    rows_ref[...] = modulated(hidden_ref[...], mods_ref[k, 0:1], mods_ref[k, 1:2]).astype(BF16)


def project(rows, w_ref):
    return [jnp.dot(rows, w_ref[part], preferred_element_type=F32) for part in range(3)]


def image_parts(query, key, value, cosine, sine, q_ref, pairs_ref):
    inner = query.shape[1]
    q_ref[...] = each_head(query, lambda v: rotated(v, cosine, sine)).astype(BF16)
    keys = each_head(key.astype(BF16).astype(F32), lambda v: rotated(v, cosine, sine))
    pairs_ref[:, :inner] = keys.astype(BF16)
    pairs_ref[:, inner:] = value.astype(BF16)


def first_project_body(
    half_ref, other_ref, w_ref, cos_ref, sin_ref, q_ref, pairs_ref, t0_ref, t1_ref
):
    rows = jnp.concatenate([half_ref[...], other_ref[...]], 0)
    parts = project(rows, w_ref)
    own = q_ref.shape[0] // 8
    each = rows.shape[0] // 8
    image = [
        jnp.concatenate([part[i * each : i * each + own] for i in range(8)], 0) for part in parts
    ]
    image_parts(*image, cos_ref[...], sin_ref[...], q_ref, pairs_ref)
    head = lax.axis_index("head")
    y_at, core = lax.div(head, 2), lax.rem(head, 2)
    key, value = [
        jnp.concatenate([part[i * each + own : (i + 1) * each] for i in range(8)], 0)
        for part in parts[1:]
    ]
    key = each_head(key, lambda v: v / jnp.sqrt(jnp.mean(v * v, -1, keepdims=True) + EPSILON))
    pairs = jnp.concatenate([key, value], -1).astype(BF16)
    count = t0_ref.shape[0]
    texts = each - own
    one = texts // STEPS
    to = lax.broadcasted_iota(jnp.int32, (STEPS * count, STEPS * count), 0)
    at = lax.broadcasted_iota(jnp.int32, (STEPS * count, STEPS * count), 1)
    goes = at % texts // one * count + head_at(at // texts, y_at, core) * one + at % one
    order = jnp.where(goes == to, 1.0, 0.0).astype(BF16)
    pairs = jnp.dot(order, pairs, preferred_element_type=F32).astype(BF16)
    t0_ref[...] = pairs[:count]
    t1_ref[...] = pairs[count:]


def project_body(half_ref, other_ref, w_ref, cos_ref, sin_ref, q_ref, pairs_ref, raw_ref):
    rows = jnp.concatenate([half_ref[...], other_ref[...]], 0)
    query, key, value = project(rows, w_ref)
    image_parts(query, key, value, cos_ref[...], sin_ref[...], q_ref, pairs_ref)
    head = lax.axis_index("head")
    y_at, core = lax.div(head, 2), lax.rem(head, 2)
    inner = q_ref.shape[1]
    tok_dev = q_ref.shape[0] // 8
    for block in range(8):
        to = pl.multiple_of(head_at(block, y_at, core) * tok_dev, tok_dev)
        lo, hi = block * tok_dev, (block + 1) * tok_dev
        raw_ref[pl.ds(to, tok_dev), :inner] = key[lo:hi].astype(BF16)
        raw_ref[pl.ds(to, tok_dev), inner:] = value[lo:hi].astype(BF16)


def attend_body(layout, q_ref, pairs_ref, stale_ref, wo_ref, *refs):
    far_refs, (keep_ref, send_ref, text_ref) = refs[:-3], refs[-3:]
    count, inner = q_ref.shape
    scale = 1.0 / math.sqrt(HEAD_DIM)
    row_micro = lax.broadcasted_iota(jnp.int32, (count, count), 0) % 16 // 8
    key_micro = lax.broadcasted_iota(jnp.int32, (count, count), 1) % 16 // 8
    at = 0
    blocks = []
    for ref, (text_first, n_text) in zip(far_refs, layout):
        rows = ref.shape[0]
        start = 0 if text_first else rows - n_text
        if n_text:
            text_ref[at : at + n_text] = ref[start : start + n_text]
            at += n_text
        if rows > n_text:
            blocks.append((ref, n_text if text_first else 0, rows - n_text, None))
    blocks.append((text_ref, 0, text_ref.shape[0], None))
    blocks.append((pairs_ref, 0, count, key_micro <= row_micro))
    blocks.append((stale_ref, 0, count, key_micro > row_micro))
    done = []
    for h in range(inner // HEAD_DIM):
        lo, hi = h * HEAD_DIM, (h + 1) * HEAD_DIM
        queries = q_ref[:, lo:hi]
        total = jnp.zeros((count, HEAD_DIM), F32)
        summed = jnp.zeros((count, HEAD_DIM), F32)
        for ref, start, rows, mask in blocks:
            scores = lax.dot_general(
                queries, ref[start : start + rows, lo:hi], (((1,), (1,)), ((), ())), preferred_element_type=F32
            )
            weights = jnp.exp(scores * scale)
            if mask is not None:
                weights = jnp.where(mask, weights, 0.0)
            for lane in range(0, rows, HEAD_DIM):
                total = total + weights[:, lane : lane + HEAD_DIM]
            summed = summed + jnp.dot(
                weights.astype(BF16),
                ref[start : start + rows, inner + lo : inner + hi],
                preferred_element_type=F32,
            )
        done.append((summed / jnp.sum(total, -1, keepdims=True)).astype(BF16))
    attended = jnp.concatenate(done, -1)
    mixed = jnp.dot(attended, wo_ref[...], preferred_element_type=F32).astype(BF16)
    keep_ref[...] = mixed[: count // 2]
    send_ref[...] = mixed[count // 2 :]


def cores_body(keep_ref, came_ref, *out_refs):
    own = out_refs[0].shape[0]
    for s, ref in enumerate(out_refs):
        at = pl.ds(s * own, own)
        ref[...] = (keep_ref[at].astype(F32) + came_ref[at].astype(F32)).astype(BF16)


def mixed_hidden(part_refs, hidden_ref, gate_row):
    mixed = part_refs[0][...].astype(F32)
    for ref in part_refs[1:]:
        mixed = mixed + ref[...].astype(F32)
    return (hidden_ref[...].astype(F32) + gate_row * mixed).astype(BF16)


def hidden_body(k, a_ref, b_ref, c_ref, d_ref, hidden_ref, mods_ref, out_ref):
    out_ref[...] = mixed_hidden([a_ref, b_ref, c_ref, d_ref], hidden_ref, mods_ref[k, 2:3])


def velocity_body(k, hidden_ref, mods_ref, w_ref, out_ref):
    rows = modulated(hidden_ref[...], mods_ref[k, 3:4], mods_ref[k, 4:5]).astype(BF16)
    out_ref[...] = lax.dot_general(
        rows, w_ref[...], (((1,), (1,)), ((), ())), preferred_element_type=F32
    )


def text_body(*refs):
    part_refs, out_ref = refs[:-1], refs[-1]
    patch = lax.axis_index("patch")
    z_at, row_at = lax.rem(patch, N_Z), lax.div(patch, N_Z)
    sources = [(0, 0), (0, 1)]
    for by in range(1, N_Z // 2):
        sources += [(-by, 0), (by, 0), (-by, 1), (by, 1)]
    sources += [(N_Z // 2, 0), (N_Z // 2, 1)]
    count = part_refs[0].shape[0]
    for ref, (by, row) in zip(part_refs, sources):
        source = lax.rem(row_at + row, 2) * N_Z + lax.rem(z_at + by + N_Z, N_Z)
        out_ref[pl.ds(pl.multiple_of(source * count, count), count)] = ref[ref.shape[0] - count :]


def ring_parts(a, b):
    parts = [b]
    up_a = down_a = a
    up_b = down_b = b
    for _ in range(N_Z // 2 - 1):
        up_a, down_a = along_z(up_a, 1), along_z(down_a, -1)
        up_b, down_b = along_z(up_b, 1), along_z(down_b, -1)
        parts += [up_a, down_a, up_b, down_b]
    return parts + [along_z(up_a, 1), along_z(down_b, -1)]


def gate(values, after):
    count = len(values)
    return list(
        pl.pallas_call(
            lambda *refs: None,
            out_shape=[jax.ShapeDtypeStruct(v.shape, v.dtype) for v in values],
            in_specs=[pl.BlockSpec(memory_space=pl.ANY)] * (count + 1),
            out_specs=[pl.BlockSpec(memory_space=pl.ANY)] * count,
            input_output_aliases={i: i for i in range(count)},
        )(*values, after)
    )


def first_ring(a, b, text, text_there):
    both = lambda *parts: jnp.concatenate(parts, 0)
    own = a.shape[0]
    ab = both(a, b)
    texts = both(text, text_there)
    count = texts.shape[0]
    up1, down1 = gate([along_z(ab, 1), along_z(ab, -1)], texts)
    up2, down2 = along_z(both(up1, texts), 1), along_z(both(texts, down1), -1)
    opposite = along_z(texts, N_Z // 2)
    up3, down3 = along_z(up2, 1), along_z(down2, -1)
    up4, down4 = along_z(up3[own:], 1), along_z(down3[: count + own], -1)
    far = [b, up1, down1, texts, opposite, up2, down2, up3, down3, up4, down4]
    return far, [(False, 0)] * 3 + [(False, count)] * 2 + [(False, count), (True, count)] * 3


def per_device(
    latent, text_states, img_in, w_qkv, w_out, w_final, mod_table, stale_cache, patch_map, timestep
):
    section = lax.axis_index("section")
    tok_dev, chan = latent.shape
    n_head = lax.axis_size("head")
    n_patch = lax.axis_size("patch")
    tok_patch = tok_dev * n_head
    width = img_in.shape[1]
    inner = w_out.shape[1]
    text_dev = text_states.shape[1]
    text_patch = text_dev * n_head
    weight = w_qkv[0].transpose(1, 0, 2)
    wo_local = w_out[0]
    final_weight = w_final.T
    rows_shape = ((tok_dev, width), BF16)
    pair_shape = ((tok_patch, 2 * inner), BF16)
    query_shape = ((tok_patch, inner), BF16)
    text_shape = ((text_patch, 2 * inner), BF16)
    angle_shape = ((tok_patch, HEAD_DIM), F32)

    stale_own, rows, hidden, mods, cosine, sine = call(
        prelude_body,
        [
            pair_shape,
            ((tok_dev + STEPS * text_dev, width), BF16),
            rows_shape,
            ((STEPS, 5, width), F32),
            angle_shape,
            angle_shape,
        ],
        timestep,
        patch_map,
        stale_cache[0].reshape(tok_patch, 2 * inner),
        latent,
        text_states[0],
        img_in,
        mod_table,
        specs=[SMEM, SMEM, VMEM, HBM, HBM, HBM, HBM],
        vmem=60,
        scratch=[
            pltpu.VMEM(latent.shape, F32),
            pltpu.VMEM(text_states.shape[1:], BF16),
            pltpu.VMEM(img_in.shape, BF16),
            pltpu.VMEM((STEPS,) + mod_table.shape[1:], BF16),
            pltpu.SemaphoreType.DMA((4,)),
        ],
    )
    stale_there = other_row(stale_own)
    half, other = gathered_heads(rows)
    queries, pairs, text0, text1 = call(
        first_project_body,
        [query_shape, pair_shape, text_shape, text_shape],
        half,
        other,
        weight,
        cosine,
        sine,
    )
    new = jnp.concatenate([pairs, text1], 0)
    there = other_row(jnp.concatenate([text0, new], 0))
    text_there, new_there = there[:text_patch], there[text_patch:]
    far, layout = first_ring(stale_own, stale_there, text0, text_there)

    def attend(k, queries, pairs, stale_pairs, far, layout, hidden):
        keep, send = call(
            functools.partial(attend_body, layout),
            [((tok_patch // 2, width), BF16)] * 2,
            queries,
            pairs,
            stale_pairs,
            wo_local,
            *far,
            scratch=[pltpu.VMEM((n_patch * text_patch, 2 * inner), BF16)],
        )
        parts = call(cores_body, [rows_shape] * N_Y, keep, other_core(send))
        parts = [parts[0]] + [along_y(parts[by], -by) for by in (1, 2, 3)]
        return call(functools.partial(hidden_body, k), rows_shape, *parts, hidden, mods)

    def stage(k, rows, hidden, stale_pairs, far, layout):
        half, other = gathered_heads(rows)
        queries, pairs, raw = call(
            project_body,
            [query_shape, pair_shape, pair_shape],
            half,
            other,
            weight,
            cosine,
            sine,
        )
        return attend(k, queries, pairs, stale_pairs, far, layout, hidden), pairs, raw

    def to_next(hidden):
        return lax.ppermute(hidden, "section", [(0, 1)])

    def normed_rows(k, hidden):
        return call(functools.partial(normed_body, k), rows_shape, hidden, mods)

    def text_of(far):
        out = call(text_body, ((n_patch * text_patch, 2 * inner), BF16), text1, *far)
        return out.reshape(1, n_patch * text_patch, 2, inner)

    def cache_of(raw):
        return raw.reshape(1, tok_patch, 2, inner)

    at_first, at_second = section == 0, section == 1
    cache_shape = [(1, tok_patch, 2, inner)]
    hidden0 = lax.cond(
        at_first,
        lambda: attend(0, queries, pairs, stale_own, far, layout, hidden),
        lambda: hidden,
    )
    hidden_in = to_next(hidden0)
    far_shapes = [new.shape] * (2 * N_Z - 1)
    far_first = lax.cond(at_first, lambda: ring_parts(new, new_there), lambda: unset(far_shapes))
    hidden_in = gate([hidden_in], far_first[0])[0]
    rows = normed_rows(0, hidden_in)

    def early_stage():
        hidden1, pairs, _ = stage(0, rows, hidden_in, stale_own, far, layout)
        new = jnp.concatenate([pairs, text1], 0)
        return hidden1, new, other_row(new)

    hidden1, new, new_there = lax.cond(
        at_second, early_stage, lambda: (hidden_in, new, new_there)
    )
    velocity0 = call(
        functools.partial(velocity_body, 0), ((tok_dev, chan), F32), hidden1, mods, final_weight
    )
    velocity_back = lax.ppermute(velocity0, "section", [(1, 0)])
    rows, hidden = call(
        entry_body,
        [rows_shape, rows_shape],
        latent,
        velocity_back,
        timestep,
        img_in,
        mods,
        specs=[VMEM, VMEM, SMEM, VMEM, VMEM],
    )
    pairs = new[:tok_patch]
    layout = [(False, text_patch)] * (2 * N_Z)

    def first_stage():
        hidden2, _, raw = stage(1, rows, hidden, pairs, far_first + [text1], layout)
        return hidden2, cache_of(raw)

    hidden2, cache = lax.cond(at_first, first_stage, lambda: (hidden, unset(cache_shape)[0]))
    hidden_in = to_next(hidden2)
    new, new_there = gate([new, new_there], hidden2)
    far_second = lax.cond(at_second, lambda: ring_parts(new, new_there), lambda: unset(far_shapes))
    hidden_in = gate([hidden_in], far_second[0])[0]
    rows = normed_rows(1, hidden_in)

    def second_stage():
        hidden3, _, raw = stage(1, rows, hidden_in, pairs, far_second + [text1], layout)
        return hidden3, cache_of(raw), text_of(far_second)

    hidden3, cache, text_out = lax.cond(
        at_second, second_stage, lambda: (hidden_in, cache, text_of(far_first))
    )
    velocity1 = call(
        functools.partial(velocity_body, 1), ((tok_dev, chan), F32), hidden3, mods, final_weight
    )
    return jnp.where(at_first, velocity_back, velocity1)[None], cache, text_out


def solution(mesh):
    return jax.shard_map(
        per_device,
        mesh=mesh,
        in_specs=(
            P(("patch", "head"), None),
            P("section", ("patch", "head"), None),
            P(),
            P("section", None, None, "head"),
            P("section", "head", None),
            P(),
            P(),
            P("section", "patch", None, "head"),
            P(),
            P(),
        ),
        out_specs=(
            P("section", ("patch", "head"), None),
            P("section", "patch", None, "head"),
            P("section", None, None, "head"),
        ),
        check_vma=False,
    )
```

```python
import functools
import math

import jax
import jax.numpy as jnp
import numpy as np
from jax import lax
from jax.experimental import pallas as pl
from jax.experimental.pallas import tpu as pltpu
from jax.sharding import PartitionSpec as P

HEAD_DIM = 128
TSTEPS = 28
COLS = 64
STEPS = 2
BLOCKS = 2
MICRO = 2
EPSILON = 1e-06
F32 = jnp.float32
BF16 = jnp.bfloat16
N_Y = 4
N_Z = 8


VMEM = pl.BlockSpec(memory_space=pltpu.VMEM)
SMEM = pl.BlockSpec(memory_space=pltpu.SMEM)
HBM = pl.BlockSpec(memory_space=pltpu.HBM)


def call(body, outs, *args, specs=None, scratch=(), vmem=16):
    single = not isinstance(outs, list)
    shapes = [outs] if single else outs
    result = pl.pallas_call(
        body,
        out_shape=[jax.ShapeDtypeStruct(shape, dtype) for shape, dtype in shapes],
        in_specs=[VMEM] * len(args) if specs is None else specs,
        out_specs=[VMEM] * len(shapes),
        scratch_shapes=list(scratch),
        compiler_params=pltpu.CompilerParams(vmem_limit_bytes=vmem * 1024 * 1024),
    )(*args)
    return result[0] if single else result


def unset(shapes):
    return list(pl.pallas_call(
        lambda *refs: None,
        out_shape=[jax.ShapeDtypeStruct(shape, BF16) for shape in shapes],
        out_specs=[pl.BlockSpec(memory_space=pl.ANY)] * len(shapes),
        compiler_params=pltpu.CompilerParams(vmem_limit_bytes=1024 * 1024),
    )())


def permuted(shard, axis, target):
    length = lax.axis_size(axis)
    return lax.ppermute(shard, axis, [(i, target(i)) for i in range(length)])


def along_y(shard, by):
    return permuted(shard, "head", lambda i: (((i >> 1) + by) % N_Y) * 2 + (i & 1))


def other_core(shard):
    return permuted(shard, "head", lambda i: i ^ 1)


def along_z(shard, by):
    return permuted(shard, "patch", lambda i: (i & N_Z) | ((i + by) % N_Z))


def other_row(shard):
    return permuted(shard, "patch", lambda i: i ^ N_Z)


def gathered_y(rows):
    return jnp.concatenate([rows] + [along_y(rows, by) for by in (1, 2, 3)], 0)


def layer_norm(values):
    centred = values - jnp.mean(values, -1, keepdims=True)
    variance = jnp.mean(centred * centred, -1, keepdims=True)
    return centred / jnp.sqrt(variance + EPSILON)


def modulated(values, shift_row, scale_row):
    return layer_norm(values.astype(F32)) * (1.0 + scale_row) + shift_row


def rotated(values, cosine, sine):
    values = values / jnp.sqrt(jnp.mean(values * values, -1, keepdims=True) + EPSILON)
    half = HEAD_DIM // 2
    swapped = jnp.concatenate([values[:, half:], values[:, :half]], -1)
    return values * cosine + swapped * sine


def each_head(values, change):
    heads = values.shape[-1] // HEAD_DIM
    return jnp.concatenate(
        [change(values[:, h * HEAD_DIM : (h + 1) * HEAD_DIM]) for h in range(heads)], -1
    )


def head_at(block, y_at, core):
    return lax.rem(y_at - block % N_Y + N_Y, N_Y) * 2 + lax.rem(core + block // N_Y, 2)


def frequencies():
    pairs_all = HEAD_DIM // 2
    fixed = pairs_all // 8
    row_pairs = (pairs_all - fixed) // 2
    col_pairs = pairs_all - fixed - row_pairs
    lane = lax.broadcasted_iota(jnp.int32, (1, HEAD_DIM), 1)
    pair = lane % pairs_all
    base = -math.log2(10000.0)
    row_freq = jnp.exp2((pair - fixed).astype(F32) * (base / row_pairs))
    col_freq = jnp.exp2((pair - fixed - row_pairs).astype(F32) * (base / col_pairs))
    in_rows = (pair >= fixed) & (pair < fixed + row_pairs)
    return (
        jnp.where(in_rows, row_freq, 0.0),
        jnp.where(pair >= fixed + row_pairs, col_freq, 0.0),
        jnp.where(lane < pairs_all, -1.0, 1.0),
    )


def prelude_body(
    step_ref,
    map_ref,
    stale_ref,
    latent_hbm,
    text_hbm,
    img_hbm,
    table_hbm,
    pairs_ref,
    rows_ref,
    hidden_ref,
    mods_ref,
    cos_ref,
    sin_ref,
    latent_ref,
    text_ref,
    img_ref,
    table_ref,
    sems,
):
    copies = [
        pltpu.make_async_copy(src, dst, sems.at[i])
        for i, (src, dst) in enumerate(
            [
                (table_hbm.at[pl.ds(step_ref[0], STEPS)], table_ref),
                (latent_hbm, latent_ref),
                (img_hbm, img_ref),
                (text_hbm, text_ref),
            ]
        )
    ]
    for copy in copies:
        copy.start()
    section, patch, head = (lax.axis_index(a) for a in ("section", "patch", "head"))
    y_at, core = lax.div(head, 2), lax.rem(head, 2)
    tok_dev = latent_ref.shape[0]
    row_freq, col_freq, sign = frequencies()
    in_block = lax.broadcasted_iota(jnp.int32, (tok_dev, HEAD_DIM), 0).astype(F32)

    def tables(head_now):
        place = map_ref[patch * 8 + head_now] * tok_dev
        grid_row = lax.div(place, COLS).astype(F32)
        column = lax.rem(place, COLS).astype(F32) + in_block
        angles = grid_row * row_freq + column * col_freq
        return jnp.cos(angles), jnp.sin(angles) * sign

    inner = stale_ref.shape[1] // 2
    for block in range(8):
        head_now = head_at(block, y_at, core)
        cosine, sine = tables(head_now)
        at = pl.ds(block * tok_dev, tok_dev)
        cos_ref[at] = cosine
        sin_ref[at] = sine
        there = pl.ds(pl.multiple_of(head_now * tok_dev, tok_dev), tok_dev)
        keys = each_head(stale_ref[there, :inner].astype(F32), lambda v: rotated(v, cosine, sine))
        pairs_ref[at, :inner] = keys.astype(BF16)
        pairs_ref[at, inner:] = stale_ref[there, inner:]
    for copy in copies:
        copy.wait()
    for k in range(STEPS):
        table = table_ref[k].astype(F32)
        mods_ref[k, 0:3] = jnp.where(section == 0, table[0:3], table[3:6])
        mods_ref[k, 3:5] = table[6:8]
    hidden = jnp.dot(latent_ref[...].astype(BF16), img_ref[...], preferred_element_type=F32)
    hidden = hidden.astype(BF16)
    hidden_ref[...] = hidden
    normed = modulated(hidden, mods_ref[0, 0:1], mods_ref[0, 1:2])
    still = layer_norm(text_ref[...].astype(F32))
    texts = [still * (1.0 + mods_ref[k, 1:2]) + mods_ref[k, 0:1] for k in range(STEPS)]
    rows_ref[...] = jnp.concatenate([normed] + texts, 0).astype(BF16)


def entry_body(latent_ref, velocity_ref, step_ref, img_ref, mods_ref, rows_ref, hidden_ref):
    first = step_ref[0].astype(F32)
    sigmas = []
    for roster in (first, first + 1.0):
        fraction = 1.0 - jnp.full(latent_ref.shape, roster) / TSTEPS
        sigmas.append(3.0 * fraction / (1.0 + 2.0 * fraction))
    latent_now = latent_ref[...] + (sigmas[1] - sigmas[0]) * velocity_ref[...]
    hidden = jnp.dot(latent_now.astype(BF16), img_ref[...], preferred_element_type=F32)
    hidden = hidden.astype(BF16)
    hidden_ref[...] = hidden
    rows_ref[...] = modulated(hidden, mods_ref[1, 0:1], mods_ref[1, 1:2]).astype(BF16)


def normed_body(k, hidden_ref, mods_ref, rows_ref):
    rows_ref[...] = modulated(hidden_ref[...], mods_ref[k, 0:1], mods_ref[k, 1:2]).astype(BF16)


def project(rows, w_ref):
    return [jnp.dot(rows, w_ref[part], preferred_element_type=F32) for part in range(3)]


def image_parts(query, key, value, cosine, sine, q_ref, pairs_ref):
    inner = query.shape[1]
    q_ref[...] = each_head(query, lambda v: rotated(v, cosine, sine)).astype(BF16)
    keys = each_head(key.astype(BF16).astype(F32), lambda v: rotated(v, cosine, sine))
    pairs_ref[:, :inner] = keys.astype(BF16)
    pairs_ref[:, inner:] = value.astype(BF16)


def first_project_body(
    half_ref, other_ref, w_ref, cos_ref, sin_ref, q_ref, pairs_ref, t0_ref, t1_ref
):
    rows = jnp.concatenate([half_ref[...], other_ref[...]], 0)
    parts = project(rows, w_ref)
    own = q_ref.shape[0] // 8
    each = rows.shape[0] // 8
    image = [
        jnp.concatenate([part[i * each : i * each + own] for i in range(8)], 0) for part in parts
    ]
    image_parts(*image, cos_ref[...], sin_ref[...], q_ref, pairs_ref)
    head = lax.axis_index("head")
    y_at, core = lax.div(head, 2), lax.rem(head, 2)
    key, value = [
        jnp.concatenate([part[i * each + own : (i + 1) * each] for i in range(8)], 0)
        for part in parts[1:]
    ]
    key = each_head(key, lambda v: v / jnp.sqrt(jnp.mean(v * v, -1, keepdims=True) + EPSILON))
    pairs = jnp.concatenate([key, value], -1).astype(BF16)
    count = t0_ref.shape[0]
    texts = each - own
    one = texts // STEPS
    to = lax.broadcasted_iota(jnp.int32, (STEPS * count, STEPS * count), 0)
    at = lax.broadcasted_iota(jnp.int32, (STEPS * count, STEPS * count), 1)
    goes = at % texts // one * count + head_at(at // texts, y_at, core) * one + at % one
    order = jnp.where(goes == to, 1.0, 0.0).astype(BF16)
    pairs = jnp.dot(order, pairs, preferred_element_type=F32).astype(BF16)
    t0_ref[...] = pairs[:count]
    t1_ref[...] = pairs[count:]


def stage_body(
    half_ref, other_ref, w_ref, cos_ref, sin_ref, stale_ref, wo_ref, *refs
):
    far_refs, refs = refs[:-7], refs[-7:]
    keep_ref, send_ref, pairs_ref, raw_ref, q_ref, kv_ref, sems = refs
    copies = []
    at = 0
    for i, ref in enumerate(far_refs):
        rows = ref.shape[0]
        copies.append(pltpu.make_async_copy(ref, kv_ref.at[pl.ds(at, rows)], sems.at[i]))
        at += rows
    for copy in copies:
        copy.start()
    rows = jnp.concatenate([half_ref[...], other_ref[...]], 0)
    query, key, value = project(rows, w_ref)
    image_parts(query, key, value, cos_ref[...], sin_ref[...], q_ref, pairs_ref)
    head = lax.axis_index("head")
    y_at, core = lax.div(head, 2), lax.rem(head, 2)
    count, inner = q_ref.shape
    tok_dev = count // 8
    for block in range(8):
        to = pl.multiple_of(head_at(block, y_at, core) * tok_dev, tok_dev)
        lo, hi = block * tok_dev, (block + 1) * tok_dev
        raw_ref[pl.ds(to, tok_dev), :inner] = key[lo:hi].astype(BF16)
        raw_ref[pl.ds(to, tok_dev), inner:] = value[lo:hi].astype(BF16)
    row_micro = lax.broadcasted_iota(jnp.int32, (count, count), 0) % 16 // 8
    key_micro = lax.broadcasted_iota(jnp.int32, (count, count), 1) % 16 // 8
    blocks = [(pairs_ref, 0, count, key_micro <= row_micro)]
    blocks += [(stale_ref, 0, count, key_micro > row_micro)]
    wide = 7 * count
    blocks += [(kv_ref, i, min(wide, at - i), None) for i in range(0, at, wide)]
    for copy in copies:
        copy.wait()
    attention(blocks, q_ref, wo_ref, keep_ref, send_ref)


def attend_body(layout, q_ref, pairs_ref, stale_ref, wo_ref, *refs):
    far_refs, (keep_ref, send_ref, text_ref) = refs[:-3], refs[-3:]
    count, inner = q_ref.shape
    scale = 1.0 / math.sqrt(HEAD_DIM)
    row_micro = lax.broadcasted_iota(jnp.int32, (count, count), 0) % 16 // 8
    key_micro = lax.broadcasted_iota(jnp.int32, (count, count), 1) % 16 // 8
    at = 0
    blocks = []
    for ref, (text_first, n_text) in zip(far_refs, layout):
        rows = ref.shape[0]
        start = 0 if text_first else rows - n_text
        if n_text:
            text_ref[at : at + n_text] = ref[start : start + n_text]
            at += n_text
        if rows > n_text:
            blocks.append((ref, n_text if text_first else 0, rows - n_text, None))
    blocks.append((text_ref, 0, text_ref.shape[0], None))
    blocks.append((pairs_ref, 0, count, key_micro <= row_micro))
    blocks.append((stale_ref, 0, count, key_micro > row_micro))
    attention(blocks, q_ref, wo_ref, keep_ref, send_ref)


def attention(blocks, q_ref, wo_ref, keep_ref, send_ref):
    count, inner = q_ref.shape
    scale = 1.0 / math.sqrt(HEAD_DIM)
    done = []
    for h in range(inner // HEAD_DIM):
        lo, hi = h * HEAD_DIM, (h + 1) * HEAD_DIM
        queries = q_ref[:, lo:hi]
        total = jnp.zeros((count, HEAD_DIM), F32)
        summed = jnp.zeros((count, HEAD_DIM), F32)
        for ref, start, rows, mask in blocks:
            scores = lax.dot_general(
                queries, ref[start : start + rows, lo:hi], (((1,), (1,)), ((), ())), preferred_element_type=F32
            )
            weights = jnp.exp(scores * scale)
            if mask is not None:
                weights = jnp.where(mask, weights, 0.0)
            for lane in range(0, rows, HEAD_DIM):
                total = total + weights[:, lane : lane + HEAD_DIM]
            summed = summed + jnp.dot(
                weights.astype(BF16),
                ref[start : start + rows, inner + lo : inner + hi],
                preferred_element_type=F32,
            )
        done.append((summed / jnp.sum(total, -1, keepdims=True)).astype(BF16))
    attended = jnp.concatenate(done, -1)
    mixed = jnp.dot(attended, wo_ref[...], preferred_element_type=F32).astype(BF16)
    keep_ref[...] = mixed[: count // 2]
    send_ref[...] = mixed[count // 2 :]


def cores_body(keep_ref, came_ref, *out_refs):
    own = out_refs[0].shape[0]
    for s, ref in enumerate(out_refs):
        at = pl.ds(s * own, own)
        ref[...] = (keep_ref[at].astype(F32) + came_ref[at].astype(F32)).astype(BF16)


def mixed_hidden(part_refs, hidden_ref, gate_row):
    mixed = part_refs[0][...].astype(F32)
    for ref in part_refs[1:]:
        mixed = mixed + ref[...].astype(F32)
    return (hidden_ref[...].astype(F32) + gate_row * mixed).astype(BF16)


def hidden_body(k, a_ref, b_ref, c_ref, d_ref, hidden_ref, mods_ref, out_ref):
    out_ref[...] = mixed_hidden([a_ref, b_ref, c_ref, d_ref], hidden_ref, mods_ref[k, 2:3])


def velocity_body(k, hidden_ref, mods_ref, w_ref, out_ref):
    rows = modulated(hidden_ref[...], mods_ref[k, 3:4], mods_ref[k, 4:5]).astype(BF16)
    out_ref[...] = lax.dot_general(
        rows, w_ref[...], (((1,), (1,)), ((), ())), preferred_element_type=F32
    )


def text_body(*refs):
    part_refs, out_ref = refs[:-1], refs[-1]
    patch = lax.axis_index("patch")
    z_at, row_at = lax.rem(patch, N_Z), lax.div(patch, N_Z)
    sources = [(0, 0), (0, 1)]
    for by in range(1, N_Z // 2):
        sources += [(-by, 0), (by, 0), (-by, 1), (by, 1)]
    sources += [(N_Z // 2, 0), (N_Z // 2, 1)]
    count = part_refs[0].shape[0]
    for ref, (by, row) in zip(part_refs, sources):
        source = lax.rem(row_at + row, 2) * N_Z + lax.rem(z_at + by + N_Z, N_Z)
        out_ref[pl.ds(pl.multiple_of(source * count, count), count)] = ref[ref.shape[0] - count :]


def ring_parts(a, b):
    parts = [b]
    up_a = down_a = a
    up_b = down_b = b
    for _ in range(N_Z // 2 - 1):
        up_a, down_a = along_z(up_a, 1), along_z(down_a, -1)
        up_b, down_b = along_z(up_b, 1), along_z(down_b, -1)
        parts += [up_a, down_a, up_b, down_b]
    return parts + [along_z(up_a, 1), along_z(down_b, -1)]


def gate(values, after):
    count = len(values)
    return list(
        pl.pallas_call(
            lambda *refs: None,
            out_shape=[jax.ShapeDtypeStruct(v.shape, v.dtype) for v in values],
            in_specs=[pl.BlockSpec(memory_space=pl.ANY)] * (count + 1),
            out_specs=[pl.BlockSpec(memory_space=pl.ANY)] * count,
            input_output_aliases={i: i for i in range(count)},
            compiler_params=pltpu.CompilerParams(vmem_limit_bytes=1024 * 1024),
        )(*values, after)
    )


def both(*parts):
    return jnp.concatenate(parts, 0)


def per_device(
    latent, text_states, img_in, w_qkv, w_out, w_final, mod_table, stale_cache, patch_map, timestep
):
    section = lax.axis_index("section")
    tok_dev, chan = latent.shape
    n_head = lax.axis_size("head")
    n_patch = lax.axis_size("patch")
    tok_patch = tok_dev * n_head
    width = img_in.shape[1]
    inner = w_out.shape[1]
    text_dev = text_states.shape[1]
    text_patch = text_dev * n_head
    weight = w_qkv[0].transpose(1, 0, 2)
    wo_local = w_out[0]
    final_weight = w_final.T
    rows_shape = ((tok_dev, width), BF16)
    pair_shape = ((tok_patch, 2 * inner), BF16)
    query_shape = ((tok_patch, inner), BF16)
    text_shape = ((text_patch, 2 * inner), BF16)
    angle_shape = ((tok_patch, HEAD_DIM), F32)

    stale_own, rows, hidden, mods, cosine, sine = call(
        prelude_body,
        [
            pair_shape,
            ((tok_dev + STEPS * text_dev, width), BF16),
            rows_shape,
            ((STEPS, 5, width), F32),
            angle_shape,
            angle_shape,
        ],
        timestep,
        patch_map,
        stale_cache[0].reshape(tok_patch, 2 * inner),
        latent,
        text_states[0],
        img_in,
        mod_table,
        specs=[SMEM, SMEM, VMEM, HBM, HBM, HBM, HBM],
        vmem=60,
        scratch=[
            pltpu.VMEM(latent.shape, F32),
            pltpu.VMEM(text_states.shape[1:], BF16),
            pltpu.VMEM(img_in.shape, BF16),
            pltpu.VMEM((STEPS,) + mod_table.shape[1:], BF16),
            pltpu.SemaphoreType.DMA((4,)),
        ],
    )
    pair_shape = ((tok_patch, 2 * inner), BF16)
    text_shape = ((text_patch, 2 * inner), BF16)
    stale_there = other_row(stale_own)
    stale_both = both(stale_own, stale_there)
    up1, down1 = along_z(stale_both, 1), along_z(stale_both, -1)
    half = gate([gathered_y(rows)], up1)[0]
    half = gate([half], down1)[0]
    other = other_core(half)
    up2, down2 = along_z(up1, 1), along_z(down1, -1)
    queries, pairs, text0, text1 = call(
        first_project_body,
        [query_shape, pair_shape, text_shape, text_shape],
        half,
        other,
        weight,
        cosine,
        sine,
    )
    text0 = gate([text0], up2)[0]
    text0 = gate([text0], down2)[0]
    texts = both(text0, other_row(text0))
    count = 2 * text_patch
    up3, down3 = along_z(both(up2, texts), 1), along_z(both(texts, down2), -1)
    texts = gate([texts], up3)[0]
    up4, down4 = along_z(up3[tok_patch:], 1), along_z(down3[: count + tok_patch], -1)
    new = gate([both(pairs, text1)], up3)[0]
    new_there = other_row(new)
    far = [stale_there, up1, down1, up2, down2, up3, down3, up4, down4, texts]
    far += [along_z(texts, by) for by in (3, -3, N_Z // 2)]
    layout = [(False, 0)] * 5 + [(False, count), (True, count)] * 2 + [(False, count)] * 4

    half_shape = ((tok_patch // 2, width), BF16)

    def mix(k, keep, send, hidden):
        parts = call(cores_body, [rows_shape] * N_Y, keep, other_core(send))
        parts = [parts[0]] + [along_y(parts[by], -by) for by in (1, 2, 3)]
        return call(functools.partial(hidden_body, k), rows_shape, *parts, hidden, mods)

    def attend(k, queries, pairs, stale_pairs, far, layout, hidden):
        keep, send = call(
            functools.partial(attend_body, layout),
            [half_shape] * 2,
            queries,
            pairs,
            stale_pairs,
            wo_local,
            *far,
            scratch=[pltpu.VMEM((n_patch * text_patch, 2 * inner), BF16)],
        )
        return mix(k, keep, send, hidden)

    def stage(k, rows, hidden, stale_pairs, far):
        half = gathered_y(rows)
        far_rows = sum(part.shape[0] for part in far)
        keep, send, pairs, raw = call(
            stage_body,
            [half_shape, half_shape, pair_shape, pair_shape],
            half,
            other_core(half),
            weight,
            cosine,
            sine,
            stale_pairs,
            wo_local,
            *far,
            specs=[VMEM] * 7 + [pl.BlockSpec(memory_space=pl.ANY)] * len(far),
            scratch=[
                pltpu.VMEM((tok_patch, inner), BF16),
                pltpu.VMEM((far_rows, 2 * inner), BF16),
                pltpu.SemaphoreType.DMA((len(far),)),
            ],
        )
        return mix(k, keep, send, hidden), pairs, raw

    def to_next(hidden):
        return lax.ppermute(hidden, "section", [(0, 1)])

    def normed_rows(k, hidden):
        return call(functools.partial(normed_body, k), rows_shape, hidden, mods)

    def text_of(far):
        out = call(text_body, ((n_patch * text_patch, 2 * inner), BF16), text1, *far)
        return out.reshape(1, n_patch * text_patch, 2, inner)

    def cache_of(raw):
        return raw.reshape(1, tok_patch, 2, inner)

    at_first, at_second = section == 0, section == 1
    cache_shape = [(1, tok_patch, 2, inner)]
    hidden0 = lax.cond(
        at_first,
        lambda: attend(0, queries, pairs, stale_own, far, layout, hidden),
        lambda: hidden,
    )
    hidden_in = to_next(hidden0)
    far_shapes = [new.shape] * (2 * N_Z - 1)
    far_first = lax.cond(at_first, lambda: ring_parts(new, new_there), lambda: unset(far_shapes))
    hidden_in = gate([hidden_in], far_first[0])[0]
    rows = normed_rows(0, hidden_in)

    def early_stage():
        hidden1, pairs, _ = stage(0, rows, hidden_in, stale_own, far)
        new = both(pairs, text1)
        return hidden1, pairs, new, other_row(new)

    hidden1, later_pairs, later, later_there = lax.cond(
        at_second,
        early_stage,
        lambda: (hidden_in, *unset([pair_shape[0], new.shape, new.shape])),
    )
    velocity0 = call(
        functools.partial(velocity_body, 0), ((tok_dev, chan), F32), hidden1, mods, final_weight
    )
    velocity_back = lax.ppermute(velocity0, "section", [(1, 0)])
    far_second = lax.cond(at_second, lambda: ring_parts(later, later_there), lambda: unset(far_shapes))
    rows, hidden = call(
        entry_body,
        [rows_shape, rows_shape],
        latent,
        velocity_back,
        timestep,
        img_in,
        mods,
        specs=[VMEM, VMEM, SMEM, VMEM, VMEM],
    )

    rows = gate([rows], far_second[0])[0]

    def first_stage():
        hidden2, _, raw = stage(1, rows, hidden, pairs, far_first + [text1])
        return hidden2, cache_of(raw)

    hidden2, cache = lax.cond(at_first, first_stage, lambda: (hidden, unset(cache_shape)[0]))
    hidden_in = to_next(hidden2)
    rows = normed_rows(1, hidden_in)

    def second_stage():
        hidden3, _, raw = stage(1, rows, hidden_in, later_pairs, far_second + [text1])
        return hidden3, cache_of(raw), text_of(far_second)

    hidden3, cache, text_out = lax.cond(
        at_second, second_stage, lambda: (hidden_in, cache, text_of(far_first))
    )
    velocity1 = call(
        functools.partial(velocity_body, 1), ((tok_dev, chan), F32), hidden3, mods, final_weight
    )
    return jnp.where(at_first, velocity_back, velocity1)[None], cache, text_out


def solution(mesh):
    return jax.shard_map(
        per_device,
        mesh=mesh,
        in_specs=(
            P(("patch", "head"), None),
            P("section", ("patch", "head"), None),
            P(),
            P("section", None, None, "head"),
            P("section", "head", None),
            P(),
            P(),
            P("section", "patch", None, "head"),
            P(),
            P(),
        ),
        out_specs=(
            P("section", ("patch", "head"), None),
            P("section", "patch", None, "head"),
            P("section", None, None, "head"),
        ),
        check_vma=False,
    )
```

```python
import functools
import math

import jax
import jax.numpy as jnp
import numpy as np
from jax import lax
from jax.experimental import pallas as pl
from jax.experimental.pallas import tpu as pltpu
from jax.sharding import PartitionSpec as P

HEAD_DIM = 128
TSTEPS = 28
COLS = 64
STEPS = 2
BLOCKS = 2
MICRO = 2
EPSILON = 1e-06
F32 = jnp.float32
BF16 = jnp.bfloat16
N_Y = 4
N_Z = 8


VMEM = pl.BlockSpec(memory_space=pltpu.VMEM)
SMEM = pl.BlockSpec(memory_space=pltpu.SMEM)
HBM = pl.BlockSpec(memory_space=pltpu.HBM)


def call(body, outs, *args, specs=None, scratch=(), vmem=16):
    single = not isinstance(outs, list)
    shapes = [outs] if single else outs
    result = pl.pallas_call(
        body,
        out_shape=[jax.ShapeDtypeStruct(shape, dtype) for shape, dtype in shapes],
        in_specs=[VMEM] * len(args) if specs is None else specs,
        out_specs=[VMEM] * len(shapes),
        scratch_shapes=list(scratch),
        compiler_params=pltpu.CompilerParams(vmem_limit_bytes=vmem * 1024 * 1024),
    )(*args)
    return result[0] if single else result


def unset(shapes):
    return list(pl.pallas_call(
        lambda *refs: None,
        out_shape=[jax.ShapeDtypeStruct(shape, BF16) for shape in shapes],
        out_specs=[pl.BlockSpec(memory_space=pl.ANY)] * len(shapes),
        compiler_params=pltpu.CompilerParams(vmem_limit_bytes=1024 * 1024),
    )())


def permuted(shard, axis, target):
    length = lax.axis_size(axis)
    return lax.ppermute(shard, axis, [(i, target(i)) for i in range(length)])


def along_y(shard, by):
    return permuted(shard, "head", lambda i: (((i >> 1) + by) % N_Y) * 2 + (i & 1))


def other_core(shard):
    return permuted(shard, "head", lambda i: i ^ 1)


def along_z(shard, by):
    return permuted(shard, "patch", lambda i: (i & N_Z) | ((i + by) % N_Z))


def other_row(shard):
    return permuted(shard, "patch", lambda i: i ^ N_Z)


def gathered_y(rows):
    return jnp.concatenate([rows] + [along_y(rows, by) for by in (1, 2, 3)], 0)


def layer_norm(values):
    centred = values - jnp.mean(values, -1, keepdims=True)
    variance = jnp.mean(centred * centred, -1, keepdims=True)
    return centred / jnp.sqrt(variance + EPSILON)


def modulated(values, shift_row, scale_row):
    return layer_norm(values.astype(F32)) * (1.0 + scale_row) + shift_row


def rotated(values, cosine, sine):
    values = values / jnp.sqrt(jnp.mean(values * values, -1, keepdims=True) + EPSILON)
    half = HEAD_DIM // 2
    swapped = jnp.concatenate([values[:, half:], values[:, :half]], -1)
    return values * cosine + swapped * sine


def each_head(values, change):
    heads = values.shape[-1] // HEAD_DIM
    return jnp.concatenate(
        [change(values[:, h * HEAD_DIM : (h + 1) * HEAD_DIM]) for h in range(heads)], -1
    )


def head_at(block, y_at, core):
    return lax.rem(y_at - block % N_Y + N_Y, N_Y) * 2 + lax.rem(core + block // N_Y, 2)


def frequencies():
    pairs_all = HEAD_DIM // 2
    fixed = pairs_all // 8
    row_pairs = (pairs_all - fixed) // 2
    col_pairs = pairs_all - fixed - row_pairs
    lane = lax.broadcasted_iota(jnp.int32, (1, HEAD_DIM), 1)
    pair = lane % pairs_all
    base = -math.log2(10000.0)
    row_freq = jnp.exp2((pair - fixed).astype(F32) * (base / row_pairs))
    col_freq = jnp.exp2((pair - fixed - row_pairs).astype(F32) * (base / col_pairs))
    in_rows = (pair >= fixed) & (pair < fixed + row_pairs)
    return (
        jnp.where(in_rows, row_freq, 0.0),
        jnp.where(pair >= fixed + row_pairs, col_freq, 0.0),
        jnp.where(lane < pairs_all, -1.0, 1.0),
    )


def prelude_body(
    step_ref,
    map_ref,
    stale_ref,
    latent_hbm,
    text_hbm,
    img_hbm,
    table_hbm,
    pairs_ref,
    rows_ref,
    hidden_ref,
    mods_ref,
    cos_ref,
    sin_ref,
    latent_ref,
    text_ref,
    img_ref,
    table_ref,
    sems,
):
    copies = [
        pltpu.make_async_copy(src, dst, sems.at[i])
        for i, (src, dst) in enumerate(
            [
                (table_hbm.at[pl.ds(step_ref[0], STEPS)], table_ref),
                (latent_hbm, latent_ref),
                (img_hbm, img_ref),
                (text_hbm, text_ref),
            ]
        )
    ]
    for copy in copies:
        copy.start()
    section, patch, head = (lax.axis_index(a) for a in ("section", "patch", "head"))
    y_at, core = lax.div(head, 2), lax.rem(head, 2)
    tok_dev = latent_ref.shape[0]
    row_freq, col_freq, sign = frequencies()
    in_block = lax.broadcasted_iota(jnp.int32, (tok_dev, HEAD_DIM), 0).astype(F32)

    def tables(head_now):
        place = map_ref[patch * 8 + head_now] * tok_dev
        grid_row = lax.div(place, COLS).astype(F32)
        column = lax.rem(place, COLS).astype(F32) + in_block
        angles = grid_row * row_freq + column * col_freq
        return jnp.cos(angles), jnp.sin(angles) * sign

    inner = stale_ref.shape[1] // 2
    for block in range(8):
        head_now = head_at(block, y_at, core)
        cosine, sine = tables(head_now)
        at = pl.ds(block * tok_dev, tok_dev)
        cos_ref[at] = cosine
        sin_ref[at] = sine
        there = pl.ds(pl.multiple_of(head_now * tok_dev, tok_dev), tok_dev)
        keys = each_head(stale_ref[there, :inner].astype(F32), lambda v: rotated(v, cosine, sine))
        pairs_ref[at, :inner] = keys.astype(BF16)
        pairs_ref[at, inner:] = stale_ref[there, inner:]
    for copy in copies:
        copy.wait()
    for k in range(STEPS):
        table = table_ref[k].astype(F32)
        mods_ref[k, 0:3] = jnp.where(section == 0, table[0:3], table[3:6])
        mods_ref[k, 3:5] = table[6:8]
    hidden = jnp.dot(latent_ref[...].astype(BF16), img_ref[...], preferred_element_type=F32)
    hidden = hidden.astype(BF16)
    hidden_ref[...] = hidden
    normed = modulated(hidden, mods_ref[0, 0:1], mods_ref[0, 1:2])
    still = layer_norm(text_ref[...].astype(F32))
    texts = [still * (1.0 + mods_ref[k, 1:2]) + mods_ref[k, 0:1] for k in range(STEPS)]
    rows_ref[...] = jnp.concatenate([normed] + texts, 0).astype(BF16)


def entry_body(latent_ref, velocity_ref, step_ref, img_ref, mods_ref, rows_ref, hidden_ref):
    first = step_ref[0].astype(F32)
    sigmas = []
    for roster in (first, first + 1.0):
        fraction = 1.0 - jnp.full(latent_ref.shape, roster) / TSTEPS
        sigmas.append(3.0 * fraction / (1.0 + 2.0 * fraction))
    latent_now = latent_ref[...] + (sigmas[1] - sigmas[0]) * velocity_ref[...]
    hidden = jnp.dot(latent_now.astype(BF16), img_ref[...], preferred_element_type=F32)
    hidden = hidden.astype(BF16)
    hidden_ref[...] = hidden
    rows_ref[...] = modulated(hidden, mods_ref[1, 0:1], mods_ref[1, 1:2]).astype(BF16)


def normed_body(k, hidden_ref, mods_ref, rows_ref):
    rows_ref[...] = modulated(hidden_ref[...], mods_ref[k, 0:1], mods_ref[k, 1:2]).astype(BF16)


def project(rows, w_ref):
    return [jnp.dot(rows, w_ref[part], preferred_element_type=F32) for part in range(3)]


def image_parts(query, key, value, cosine, sine, q_ref, pairs_ref):
    inner = query.shape[1]
    q_ref[...] = each_head(query, lambda v: rotated(v, cosine, sine)).astype(BF16)
    keys = each_head(key.astype(BF16).astype(F32), lambda v: rotated(v, cosine, sine))
    pairs_ref[:, :inner] = keys.astype(BF16)
    pairs_ref[:, inner:] = value.astype(BF16)


def first_project_body(
    half_ref, other_ref, w_ref, cos_ref, sin_ref, q_ref, pairs_ref, t0_ref, t1_ref
):
    rows = jnp.concatenate([half_ref[...], other_ref[...]], 0)
    parts = project(rows, w_ref)
    own = q_ref.shape[0] // 8
    each = rows.shape[0] // 8
    image = [
        jnp.concatenate([part[i * each : i * each + own] for i in range(8)], 0) for part in parts
    ]
    image_parts(*image, cos_ref[...], sin_ref[...], q_ref, pairs_ref)
    head = lax.axis_index("head")
    y_at, core = lax.div(head, 2), lax.rem(head, 2)
    key, value = [
        jnp.concatenate([part[i * each + own : (i + 1) * each] for i in range(8)], 0)
        for part in parts[1:]
    ]
    key = each_head(key, lambda v: v / jnp.sqrt(jnp.mean(v * v, -1, keepdims=True) + EPSILON))
    pairs = jnp.concatenate([key, value], -1).astype(BF16)
    count = t0_ref.shape[0]
    texts = each - own
    one = texts // STEPS
    to = lax.broadcasted_iota(jnp.int32, (STEPS * count, STEPS * count), 0)
    at = lax.broadcasted_iota(jnp.int32, (STEPS * count, STEPS * count), 1)
    goes = at % texts // one * count + head_at(at // texts, y_at, core) * one + at % one
    order = jnp.where(goes == to, 1.0, 0.0).astype(BF16)
    pairs = jnp.dot(order, pairs, preferred_element_type=F32).astype(BF16)
    t0_ref[...] = pairs[:count]
    t1_ref[...] = pairs[count:]


def stage_body(
    half_ref, other_ref, w_ref, cos_ref, sin_ref, stale_ref, wo_ref, *refs
):
    far_refs, refs = refs[:-7], refs[-7:]
    keep_ref, send_ref, pairs_ref, raw_ref, q_ref, kv_ref, sems = refs
    copies = []
    at = 0
    for i, ref in enumerate(far_refs):
        rows = ref.shape[0]
        copies.append(pltpu.make_async_copy(ref, kv_ref.at[pl.ds(at, rows)], sems.at[i]))
        at += rows
    for copy in copies:
        copy.start()
    rows = jnp.concatenate([half_ref[...], other_ref[...]], 0)
    query, key, value = project(rows, w_ref)
    image_parts(query, key, value, cos_ref[...], sin_ref[...], q_ref, pairs_ref)
    head = lax.axis_index("head")
    y_at, core = lax.div(head, 2), lax.rem(head, 2)
    count, inner = q_ref.shape
    tok_dev = count // 8
    for block in range(8):
        to = pl.multiple_of(head_at(block, y_at, core) * tok_dev, tok_dev)
        lo, hi = block * tok_dev, (block + 1) * tok_dev
        raw_ref[pl.ds(to, tok_dev), :inner] = key[lo:hi].astype(BF16)
        raw_ref[pl.ds(to, tok_dev), inner:] = value[lo:hi].astype(BF16)
    row_micro = lax.broadcasted_iota(jnp.int32, (count, count), 0) % 16 // 8
    key_micro = lax.broadcasted_iota(jnp.int32, (count, count), 1) % 16 // 8
    blocks = [(pairs_ref, 0, count, key_micro <= row_micro)]
    blocks += [(stale_ref, 0, count, key_micro > row_micro)]
    wide = 7 * count
    blocks += [(kv_ref, i, min(wide, at - i), None) for i in range(0, at, wide)]
    for copy in copies:
        copy.wait()
    attention(blocks, q_ref, wo_ref, keep_ref, send_ref)


def attend_body(layout, q_ref, pairs_ref, stale_ref, wo_ref, *refs):
    far_refs, (keep_ref, send_ref, text_ref) = refs[:-3], refs[-3:]
    count, inner = q_ref.shape
    scale = 1.0 / math.sqrt(HEAD_DIM)
    row_micro = lax.broadcasted_iota(jnp.int32, (count, count), 0) % 16 // 8
    key_micro = lax.broadcasted_iota(jnp.int32, (count, count), 1) % 16 // 8
    at = 0
    blocks = []
    for ref, (text_first, n_text) in zip(far_refs, layout):
        rows = ref.shape[0]
        start = 0 if text_first else rows - n_text
        if n_text:
            text_ref[at : at + n_text] = ref[start : start + n_text]
            at += n_text
        if rows > n_text:
            blocks.append((ref, n_text if text_first else 0, rows - n_text, None))
    blocks.append((text_ref, 0, text_ref.shape[0], None))
    blocks.append((pairs_ref, 0, count, key_micro <= row_micro))
    blocks.append((stale_ref, 0, count, key_micro > row_micro))
    attention(blocks, q_ref, wo_ref, keep_ref, send_ref)


def attention(blocks, q_ref, wo_ref, keep_ref, send_ref):
    count, inner = q_ref.shape
    scale = 1.0 / math.sqrt(HEAD_DIM)
    done = []
    for h in range(inner // HEAD_DIM):
        lo, hi = h * HEAD_DIM, (h + 1) * HEAD_DIM
        queries = q_ref[:, lo:hi]
        total = jnp.zeros((count, HEAD_DIM), F32)
        summed = jnp.zeros((count, HEAD_DIM), F32)
        for ref, start, rows, mask in blocks:
            scores = lax.dot_general(
                queries, ref[start : start + rows, lo:hi], (((1,), (1,)), ((), ())), preferred_element_type=F32
            )
            weights = jnp.exp(scores * scale)
            if mask is not None:
                weights = jnp.where(mask, weights, 0.0)
            for lane in range(0, rows, HEAD_DIM):
                total = total + weights[:, lane : lane + HEAD_DIM]
            summed = summed + jnp.dot(
                weights.astype(BF16),
                ref[start : start + rows, inner + lo : inner + hi],
                preferred_element_type=F32,
            )
        done.append((summed / jnp.sum(total, -1, keepdims=True)).astype(BF16))
    attended = jnp.concatenate(done, -1)
    mixed = jnp.dot(attended, wo_ref[...], preferred_element_type=F32).astype(BF16)
    keep_ref[...] = mixed[: count // 2]
    send_ref[...] = mixed[count // 2 :]


def cores_body(keep_ref, came_ref, *out_refs):
    own = out_refs[0].shape[0]
    for s, ref in enumerate(out_refs):
        at = pl.ds(s * own, own)
        ref[...] = (keep_ref[at].astype(F32) + came_ref[at].astype(F32)).astype(BF16)


def mixed_hidden(part_refs, hidden_ref, gate_row):
    mixed = part_refs[0][...].astype(F32)
    for ref in part_refs[1:]:
        mixed = mixed + ref[...].astype(F32)
    return (hidden_ref[...].astype(F32) + gate_row * mixed).astype(BF16)


def hidden_body(k, a_ref, b_ref, c_ref, d_ref, hidden_ref, mods_ref, out_ref):
    out_ref[...] = mixed_hidden([a_ref, b_ref, c_ref, d_ref], hidden_ref, mods_ref[k, 2:3])


def velocity_body(k, hidden_ref, mods_ref, w_ref, out_ref):
    rows = modulated(hidden_ref[...], mods_ref[k, 3:4], mods_ref[k, 4:5]).astype(BF16)
    out_ref[...] = lax.dot_general(
        rows, w_ref[...], (((1,), (1,)), ((), ())), preferred_element_type=F32
    )


def text_body(*refs):
    part_refs, out_ref = refs[:-1], refs[-1]
    patch = lax.axis_index("patch")
    z_at, row_at = lax.rem(patch, N_Z), lax.div(patch, N_Z)
    sources = [(0, 0), (0, 1)]
    for by in range(1, N_Z // 2):
        sources += [(-by, 0), (by, 0), (-by, 1), (by, 1)]
    sources += [(N_Z // 2, 0), (N_Z // 2, 1)]
    count = part_refs[0].shape[0]
    for ref, (by, row) in zip(part_refs, sources):
        source = lax.rem(row_at + row, 2) * N_Z + lax.rem(z_at + by + N_Z, N_Z)
        out_ref[pl.ds(pl.multiple_of(source * count, count), count)] = ref[ref.shape[0] - count :]


def ring_parts(a, b):
    parts = [b]
    up_a = down_a = a
    up_b = down_b = b
    for _ in range(N_Z // 2 - 1):
        up_a, down_a = along_z(up_a, 1), along_z(down_a, -1)
        up_b, down_b = along_z(up_b, 1), along_z(down_b, -1)
        parts += [up_a, down_a, up_b, down_b]
    return parts + [along_z(up_a, 1), along_z(down_b, -1)]


def gate(values, after):
    count = len(values)
    return list(
        pl.pallas_call(
            lambda *refs: None,
            out_shape=[jax.ShapeDtypeStruct(v.shape, v.dtype) for v in values],
            in_specs=[pl.BlockSpec(memory_space=pl.ANY)] * (count + 1),
            out_specs=[pl.BlockSpec(memory_space=pl.ANY)] * count,
            input_output_aliases={i: i for i in range(count)},
            compiler_params=pltpu.CompilerParams(vmem_limit_bytes=1024 * 1024),
        )(*values, after)
    )


def both(*parts):
    return jnp.concatenate(parts, 0)


def per_device(
    latent, text_states, img_in, w_qkv, w_out, w_final, mod_table, stale_cache, patch_map, timestep
):
    section = lax.axis_index("section")
    tok_dev, chan = latent.shape
    n_head = lax.axis_size("head")
    n_patch = lax.axis_size("patch")
    tok_patch = tok_dev * n_head
    width = img_in.shape[1]
    inner = w_out.shape[1]
    text_dev = text_states.shape[1]
    text_patch = text_dev * n_head
    weight = w_qkv[0].transpose(1, 0, 2)
    wo_local = w_out[0]
    final_weight = w_final.T
    rows_shape = ((tok_dev, width), BF16)
    pair_shape = ((tok_patch, 2 * inner), BF16)
    query_shape = ((tok_patch, inner), BF16)
    text_shape = ((text_patch, 2 * inner), BF16)
    angle_shape = ((tok_patch, HEAD_DIM), F32)

    stale_own, rows, hidden, mods, cosine, sine = call(
        prelude_body,
        [
            pair_shape,
            ((tok_dev + STEPS * text_dev, width), BF16),
            rows_shape,
            ((STEPS, 5, width), F32),
            angle_shape,
            angle_shape,
        ],
        timestep,
        patch_map,
        stale_cache[0].reshape(tok_patch, 2 * inner),
        latent,
        text_states[0],
        img_in,
        mod_table,
        specs=[SMEM, SMEM, VMEM, HBM, HBM, HBM, HBM],
        vmem=60,
        scratch=[
            pltpu.VMEM(latent.shape, F32),
            pltpu.VMEM(text_states.shape[1:], BF16),
            pltpu.VMEM(img_in.shape, BF16),
            pltpu.VMEM((STEPS,) + mod_table.shape[1:], BF16),
            pltpu.SemaphoreType.DMA((4,)),
        ],
    )
    pair_shape = ((tok_patch, 2 * inner), BF16)
    text_shape = ((text_patch, 2 * inner), BF16)
    stale_there = other_row(stale_own)
    stale_both = both(stale_own, stale_there)
    up1, down1 = along_z(stale_both, 1), along_z(stale_both, -1)
    half = gate([gathered_y(rows)], up1)[0]
    half = gate([half], down1)[0]
    other = other_core(half)
    up2, down2 = along_z(up1, 1), along_z(down1, -1)
    queries, pairs, text0, text1 = call(
        first_project_body,
        [query_shape, pair_shape, text_shape, text_shape],
        half,
        other,
        weight,
        cosine,
        sine,
    )
    text0 = gate([text0], up2)[0]
    text0 = gate([text0], down2)[0]
    texts = both(text0, other_row(text0))
    count = 2 * text_patch
    up3, down3 = along_z(both(up2, texts), 1), along_z(both(texts, down2), -1)
    texts = gate([texts], up3)[0]
    up4, down4 = along_z(up3[tok_patch:], 1), along_z(down3[: count + tok_patch], -1)
    new = gate([both(pairs, text1)], up3)[0]
    new_there = other_row(new)
    far = [stale_there, up1, down1, up2, down2, up3, down3, up4, down4, texts]
    two_texts = both(texts, up3[2 * tok_patch :])
    far += [along_z(two_texts, 3), along_z(texts, -3)]
    layout = [(False, 0)] * 5 + [(False, count), (True, count)] * 2
    layout += [(False, count), (False, 2 * count), (False, count)]

    half_shape = ((tok_patch // 2, width), BF16)

    def mix(k, keep, send, hidden):
        parts = call(cores_body, [rows_shape] * N_Y, keep, other_core(send))
        parts = [parts[0]] + [along_y(parts[by], -by) for by in (1, 2, 3)]
        return call(functools.partial(hidden_body, k), rows_shape, *parts, hidden, mods)

    def attend(k, queries, pairs, stale_pairs, far, layout, hidden):
        keep, send = call(
            functools.partial(attend_body, layout),
            [half_shape] * 2,
            queries,
            pairs,
            stale_pairs,
            wo_local,
            *far,
            scratch=[pltpu.VMEM((n_patch * text_patch, 2 * inner), BF16)],
        )
        return mix(k, keep, send, hidden)

    def stage(k, rows, hidden, stale_pairs, far):
        half = gathered_y(rows)
        far_rows = sum(part.shape[0] for part in far)
        keep, send, pairs, raw = call(
            stage_body,
            [half_shape, half_shape, pair_shape, pair_shape],
            half,
            other_core(half),
            weight,
            cosine,
            sine,
            stale_pairs,
            wo_local,
            *far,
            specs=[VMEM] * 7 + [pl.BlockSpec(memory_space=pl.ANY)] * len(far),
            scratch=[
                pltpu.VMEM((tok_patch, inner), BF16),
                pltpu.VMEM((far_rows, 2 * inner), BF16),
                pltpu.SemaphoreType.DMA((len(far),)),
            ],
        )
        return mix(k, keep, send, hidden), pairs, raw

    def to_next(hidden):
        return lax.ppermute(hidden, "section", [(0, 1)])

    def normed_rows(k, hidden):
        return call(functools.partial(normed_body, k), rows_shape, hidden, mods)

    def text_of(far):
        out = call(text_body, ((n_patch * text_patch, 2 * inner), BF16), text1, *far)
        return out.reshape(1, n_patch * text_patch, 2, inner)

    def cache_of(raw):
        return raw.reshape(1, tok_patch, 2, inner)

    at_first, at_second = section == 0, section == 1
    cache_shape = [(1, tok_patch, 2, inner)]
    hidden0 = lax.cond(
        at_first,
        lambda: attend(0, queries, pairs, stale_own, far, layout, hidden),
        lambda: hidden,
    )
    hidden_in = to_next(hidden0)
    far_shapes = [new.shape] * (2 * N_Z - 1)
    far_first = lax.cond(at_first, lambda: ring_parts(new, new_there), lambda: unset(far_shapes))
    hidden_in = gate([hidden_in], far_first[0])[0]

    velocity_shape = ((tok_dev, chan), F32)

    def velocity_of(k, hidden):
        return call(
            functools.partial(velocity_body, k), velocity_shape, hidden, mods, final_weight
        )

    def early_stage():
        rows = normed_rows(0, hidden_in)
        hidden1, pairs, _ = stage(0, rows, hidden_in, stale_own, far)
        new = both(pairs, text1)
        return velocity_of(0, hidden1), pairs, new, other_row(new)

    velocity0, later_pairs, later, later_there = lax.cond(
        at_second,
        early_stage,
        lambda: (
            jnp.zeros(*velocity_shape),
            *unset([pair_shape[0], new.shape, new.shape]),
        ),
    )
    velocity_back = lax.ppermute(velocity0, "section", [(1, 0)])
    far_second = lax.cond(at_second, lambda: ring_parts(later, later_there), lambda: unset(far_shapes))
    rows, hidden = call(
        entry_body,
        [rows_shape, rows_shape],
        latent,
        velocity_back,
        timestep,
        img_in,
        mods,
        specs=[VMEM, VMEM, SMEM, VMEM, VMEM],
    )

    rows = gate([rows], far_second[0])[0]

    def first_stage():
        hidden2, _, raw = stage(1, rows, hidden, pairs, far_first + [text1])
        return hidden2, cache_of(raw)

    hidden2, cache = lax.cond(at_first, first_stage, lambda: (hidden, unset(cache_shape)[0]))
    hidden_in = to_next(hidden2)
    rows = normed_rows(1, hidden_in)

    def second_stage():
        hidden3, _, raw = stage(1, rows, hidden_in, later_pairs, far_second + [text1])
        return hidden3, cache_of(raw), text_of(far_second)

    hidden3, cache, text_out = lax.cond(
        at_second, second_stage, lambda: (hidden_in, cache, text_of(far_first))
    )
    velocity1 = velocity_of(1, hidden3)
    return jnp.where(at_first, velocity_back, velocity1)[None], cache, text_out


def solution(mesh):
    return jax.shard_map(
        per_device,
        mesh=mesh,
        in_specs=(
            P(("patch", "head"), None),
            P("section", ("patch", "head"), None),
            P(),
            P("section", None, None, "head"),
            P("section", "head", None),
            P(),
            P(),
            P("section", "patch", None, "head"),
            P(),
            P(),
        ),
        out_specs=(
            P("section", ("patch", "head"), None),
            P("section", "patch", None, "head"),
            P("section", None, None, "head"),
        ),
        check_vma=False,
    )
```
